512 devices in a mesh: seq: 32 (over z, y_lo), head: 4 (over x), user: 4 (over y_hi, core).
Axes of the slice: x: 4, y: 8 (y_hi: 2, y_lo: 4; y = y_hi * 4 + y_lo), z: 8, core: 2. Of those that a mesh axis runs over, the one named last changes fastest.
Arguments:
- cand_rows: bfloat16 [8192, 1024], P(('user', 'seq'), 'head'), parts along dimension 0, may hold values from -6 to 6
- qu_weight: bfloat16 [1024, 2, 1024], P(None, None, 'head'), may hold values from -0.1875 to 0.1875
- out_weight: bfloat16 [1024, 1024], P('head'), may hold values from -0.1875 to 0.1875
- keys: bfloat16 [8, 32768, 1024], P('user', 'seq', 'head'), parts along dimension 0, may hold values from -6 to 6
- values: bfloat16 [8, 32768, 1024], P('user', 'seq', 'head'), parts along dimension 0, may hold values from -6 to 6
- lengths: int32 [8], P('user'), parts along dimension 0, may hold values from 1 to 32768, as said below
- cand_user: int32 [8192], P(('user', 'seq')), parts along dimension 0, may hold values from 0 to 1, as said below
Outputs:
- mixed: bfloat16 [8192, 1024], P(('user', 'seq'), 'head'), parts along dimension 0
The draws below stay inside these ranges and needn't reach their ends.
There are 4 independent parts, one for each index of `user`. The reference program is written for one: setup_inputs(seed, part) draws one part's arguments, and reference() takes and returns one part's arrays. A program takes and returns all parts, laid end to end along the dimension named above; an argument that names none is the same for every part. Nothing has to cross between parts.
Inputs may be any that keep to these rules, and one draw needn't show every extreme that they name: `lengths`: exactly one user of each part has 32768 positions, the others fewer. `cand_user`: each aligned block of 64 rows (the rows of one index of seq) holds exactly 32 rows of each user.
All inputs are finite; a program needn't handle non-finite values.
Results may differ from the reference program's by a relative error of at most 0.0047.
Values may be sent and summed in bfloat16 or wider, within the bound.
No kernel may reach another device: no remote copies, remote signals or barrier semaphores. Data moves between devices by JAX's collectives and lax.ppermute only.
A program may use at most 64 MiB of HBM per device.

```python
import math
import jax
import jax.numpy as jnp
from jax import lax

D = 1024
HEADS = 16
HEAD_DIM = 64
USERS = 2
CAND_DEV = 64
CANDS = 2048
HIST = 32768


def draw_lengths(key, part):
    key = jax.random.fold_in(key, 11)
    first_key, second_key = jax.random.split(key)
    drawn = jax.random.randint(first_key, (USERS,), 1, HIST)
    longest = jax.random.randint(second_key, (), 0, USERS)
    return jnp.where(jnp.arange(USERS) == longest, HIST, drawn).astype(jnp.int32)


def draw_cand_user(key, part):
    key = jax.random.fold_in(key, 13)
    block_total = CANDS // CAND_DEV
    base = (jnp.arange(CAND_DEV, dtype=jnp.int32) % USERS).astype(jnp.int32)
    block_keys = jax.random.split(key, block_total)

    def shuffle_block(block_key):
        return jax.random.permutation(block_key, base)
    shuffled = jax.vmap(shuffle_block)(block_keys)
    return shuffled.reshape(CANDS).astype(jnp.int32)


def block_scale(own_key, shape, cuts, least, high):
    loudness, own = 1.0, jax.random.fold_in(own_key, 6)
    for dim, shards_of in cuts:
        heights = jnp.exp(jax.random.uniform(jax.random.fold_in(own, dim), (shards_of,), jnp.float32, least / len(cuts), high / len(cuts)))
        loudness = loudness * jnp.repeat(heights, shape[dim] // shards_of).reshape([-1 if axis == dim else 1 for axis in range(len(shape))])
    return loudness


def bell_draw(rng, dims, deviation, most, shards=(), kind=jnp.bfloat16):
    values = deviation * jax.random.normal(rng, dims, jnp.float32)
    if shards:
        values = values * block_scale(rng, dims, shards, -0.22, 0.18)
    return jnp.clip(values, -most, most).astype(kind)


def setup_inputs(seed: int = 0, part: int = 0) -> dict:
    seeds = jax.random.split(jax.random.key(seed), 8)
    part_keys = jax.random.split(jax.random.fold_in(seeds[7], part), 8)
    return {
        "cand_rows": bell_draw(part_keys[0], (CANDS, D), 1.0, 6.0, ((0, 32), (1, 4))),
        "qu_weight": bell_draw(seeds[1], (D, 2, D), D ** -0.5, 0.1875, ((2, 4),)),
        "out_weight": bell_draw(seeds[2], (D, D), D ** -0.5, 0.1875, ((0, 4),)),
        "keys": bell_draw(part_keys[3], (USERS, HIST, D), 1.0, 6.0, ((1, 32), (2, 4))),
        "values": bell_draw(part_keys[4], (USERS, HIST, D), 1.0, 6.0, ((1, 32), (2, 4))),
        "lengths": draw_lengths(jax.random.fold_in(jax.random.fold_in(seeds[7], part), 71), part),
        "cand_user": draw_cand_user(jax.random.fold_in(jax.random.fold_in(seeds[7], part), 71), part),
    }


def reference(cand_rows, qu_weight, out_weight, keys, values, lengths, cand_user):
    projected = jax.nn.silu(jnp.dot(cand_rows, qu_weight.reshape(D, 2 * D), preferred_element_type=jnp.float32))
    queries = projected[:, :D].astype(jnp.bfloat16)
    gate_rows = projected[:, D:].astype(jnp.bfloat16)
    query_heads = queries.reshape(CANDS, HEADS, HEAD_DIM)
    key_heads = keys.reshape(USERS, HIST, HEADS, HEAD_DIM)
    value_heads = values.reshape(USERS, HIST, HEADS, HEAD_DIM)
    block_size = math.gcd(HIST, 2048)
    block_count = HIST // block_size
    scale = HEAD_DIM ** (-0.5)

    def one_head(head_id):
        query_now = query_heads[:, head_id, :]
        totals = jnp.zeros((CANDS, HEAD_DIM), jnp.float32)
        for owner_id in range(USERS):
            key_blocks = key_heads[owner_id, :, head_id, :].reshape(block_count, block_size, HEAD_DIM)
            value_blocks = value_heads[owner_id, :, head_id, :].reshape(block_count, block_size, HEAD_DIM)
            row_match = cand_user == owner_id

            def visit(running, inputs):
                key_block, value_block, block_id = inputs
                scores = jnp.dot(query_now, key_block.T, preferred_element_type=jnp.float32) * scale
                position = block_id * block_size + jnp.arange(block_size, dtype=jnp.int32)
                keeper = row_match[:, None] & (position < lengths[owner_id])[None, :]
                weight = jnp.where(keeper, jax.nn.silu(scores), 0.0).astype(jnp.bfloat16)
                return (running + jnp.dot(weight, value_block, preferred_element_type=jnp.float32), None)
            totals, _ = lax.scan(visit, totals, (key_blocks, value_blocks, jnp.arange(block_count, dtype=jnp.int32)))
        return totals
    gathered = lax.map(one_head, jnp.arange(HEADS, dtype=jnp.int32))
    totals = jnp.transpose(gathered, (1, 0, 2))
    row_lengths = lengths[cand_user].astype(jnp.float32)
    attn = totals / row_lengths[:, None, None]
    normed = attn * lax.rsqrt(lax.optimization_barrier(jnp.mean(attn * attn, axis=-1, keepdims=True)) + 1e-06)
    gated = (normed.reshape(CANDS, D) * gate_rows.astype(jnp.float32)).astype(jnp.bfloat16)
    product = jnp.dot(gated, out_weight, preferred_element_type=jnp.float32)
    return (cand_rows.astype(jnp.float32) + product).astype(jnp.bfloat16)
```

```python
import functools

import jax
import jax.numpy as jnp
from jax import lax
from jax.experimental import pallas as pl
from jax.experimental.pallas import tpu as pltpu
from jax.sharding import PartitionSpec as P

HEAD_DIM = 64
USERS = 2
VMEM = pl.BlockSpec(memory_space=pltpu.VMEM)
SMEM = pl.BlockSpec(memory_space=pltpu.SMEM)
PARAMS = pltpu.CompilerParams(vmem_limit_bytes=48 * 2**20)


def head_mask(shape, head):
    lane = lax.broadcasted_iota(jnp.int32, shape, len(shape) - 1)
    return (lane >= head * HEAD_DIM) & (lane < (head + 1) * HEAD_DIM)


def project_kernel(user_ref, cand_ref, weight_ref, query_ref, gate_ref):
    slices, rows, depth = cand_ref.shape
    width = weight_ref.shape[1] // 2
    total = jnp.zeros((rows, 2 * width), jnp.float32)
    for part in range(slices):
        total += jnp.dot(
            cand_ref[part],
            weight_ref[part * depth : (part + 1) * depth, :],
            preferred_element_type=jnp.float32,
        )
    projected = total / (1.0 + jnp.exp(-total))
    first = lax.broadcasted_iota(jnp.int32, (rows, rows), 0)
    second = lax.broadcasted_iota(jnp.int32, (rows, rows), 1)
    users = jnp.broadcast_to(user_ref[...], (rows, rows)).astype(jnp.bfloat16)
    before = jnp.dot(
        users, (first < second).astype(jnp.bfloat16), preferred_element_type=jnp.float32
    ).astype(jnp.int32)
    target = jnp.where(users > 0, rows // USERS + before, second - before)
    place = (target == first).astype(jnp.bfloat16)
    ordered = jnp.dot(
        place, projected.astype(jnp.bfloat16), preferred_element_type=jnp.float32
    )
    query = (ordered[:, :width] * (0.5 * HEAD_DIM**-0.5)).astype(jnp.bfloat16)
    for copy in range(query_ref.shape[0]):
        query_ref[copy] = query
    gate_ref[...] = ordered[:, width:].astype(jnp.bfloat16)


def attend_kernel(
    rows_now, positions_now, live_ref, query_ref, key_ref, value_ref, out_ref, keys, masked
):
    blocks, block_rows, width = query_ref.shape
    heads = width // HEAD_DIM
    positions = key_ref.shape[1]
    per_user = block_rows // USERS
    step_blocks = rows_now // per_user
    for user in range(USERS):
        keys[user] = key_ref[user].T
        position = lax.broadcasted_iota(jnp.int32, (positions, width), 0)
        value = value_ref[user]
        for head in range(heads):
            keep = (position < live_ref[user]) & head_mask((positions, width), head)
            masked[user, head * positions : (head + 1) * positions, :] = jnp.where(
                keep, value, jnp.zeros_like(value)
            )

        def step(index, carry, user=user):
            here = pl.ds(index * step_blocks, step_blocks)
            mine = slice(user * per_user, (user + 1) * per_user)
            query = query_ref[here, mine, :].reshape(rows_now, width)
            total = jnp.zeros((rows_now, width), jnp.float32)
            for start in range(0, positions, positions_now):
                for head in range(heads):
                    own = jnp.where(
                        head_mask((rows_now, width), head), query, jnp.zeros_like(query)
                    )
                    half = jnp.dot(
                        own,
                        keys[user, :, start : start + positions_now],
                        preferred_element_type=jnp.float32,
                    )
                    weight = (half + half * jnp.tanh(half)).astype(jnp.bfloat16)
                    at = head * positions + start
                    total += jnp.dot(
                        weight,
                        masked[user, at : at + positions_now, :],
                        preferred_element_type=jnp.float32,
                    )
            out_ref[here, mine, :] = total.astype(jnp.bfloat16).reshape(
                step_blocks, per_user, width
            )
            return carry

        lax.fori_loop(0, blocks // step_blocks, step, 0)


def finish_kernel(length_ref, user_ref, partial_ref, gate_ref, weight_ref, out_ref):
    blocks, rows, width = partial_ref.shape
    total = partial_ref[0].astype(jnp.float32)
    for block in range(1, blocks):
        total += partial_ref[block].astype(jnp.float32)
    row = lax.broadcasted_iota(jnp.int32, (rows, width), 0)
    length = jnp.where(row < rows // USERS, length_ref[0], length_ref[1]).astype(jnp.float32)
    attn = total / length
    square = attn * attn
    mean = jnp.zeros((rows, width), jnp.float32)
    for head in range(width // HEAD_DIM):
        mask = head_mask((rows, width), head)
        summed = jnp.sum(jnp.where(mask, square, 0.0), axis=1, keepdims=True)
        mean = jnp.where(mask, summed * (1.0 / HEAD_DIM), mean)
    normed = attn * lax.rsqrt(mean + 1e-06)
    gated = (normed * gate_ref[...].astype(jnp.float32)).astype(jnp.bfloat16)
    first = lax.broadcasted_iota(jnp.int32, (rows, rows), 0)
    second = lax.broadcasted_iota(jnp.int32, (rows, rows), 1)
    users = jnp.broadcast_to(user_ref[...], (rows, rows)).astype(jnp.bfloat16)
    before = jnp.dot(
        (second < first).astype(jnp.bfloat16), users, preferred_element_type=jnp.float32
    ).astype(jnp.int32)
    target = jnp.where(users > 0, rows // USERS + before, first - before)
    back = (target == second).astype(jnp.bfloat16)
    gated = jnp.dot(back, gated, preferred_element_type=jnp.float32).astype(jnp.bfloat16)
    for part in range(out_ref.shape[0]):
        out_ref[part] = jnp.dot(
            gated,
            weight_ref[:, part * width : (part + 1) * width],
            preferred_element_type=jnp.float32,
        )


def local(cand_rows, qu_weight, out_weight, keys, values, lengths, cand_user):
    rows, depth = cand_rows.shape
    width = qu_weight.shape[2]
    positions = keys.shape[1]
    groups = lax.axis_size("head")
    owners = lax.axis_size("seq")
    first_position = lax.axis_index("seq") * positions
    live = jnp.clip(lengths - first_position, 0, positions).astype(jnp.int32)

    copies = jnp.broadcast_to(cand_rows[None], (groups, rows, depth))
    cand_parts = lax.all_to_all(copies, "head", 0, 0, tiled=True)
    queries, gates = pl.pallas_call(
        project_kernel,
        out_shape=(
            jax.ShapeDtypeStruct((owners, rows, width), jnp.bfloat16),
            jax.ShapeDtypeStruct((rows, width), jnp.bfloat16),
        ),
        in_specs=[VMEM] * 3,
        out_specs=(VMEM, VMEM),
        compiler_params=PARAMS,
        name="project",
    )(
        cand_user.reshape(1, rows),
        cand_parts,
        qu_weight.reshape(qu_weight.shape[0], 2 * width),
    )
    queries = lax.all_to_all(queries, "seq", 0, 0, tiled=True)
    totals = pl.pallas_call(
        functools.partial(attend_kernel, 512, 256),
        out_shape=jax.ShapeDtypeStruct((owners, rows, width), jnp.bfloat16),
        in_specs=[SMEM] + [VMEM] * 3,
        out_specs=VMEM,
        scratch_shapes=[
            pltpu.VMEM((USERS, width, positions), jnp.bfloat16),
            pltpu.VMEM((USERS, width // HEAD_DIM * positions, width), jnp.bfloat16),
        ],
        compiler_params=PARAMS,
        name="attend",
    )(live, queries, keys, values)
    totals = lax.all_to_all(totals, "seq", 0, 0, tiled=True)
    terms = pl.pallas_call(
        finish_kernel,
        out_shape=jax.ShapeDtypeStruct((groups, rows, depth), jnp.float32),
        in_specs=[SMEM] + [VMEM] * 4,
        out_specs=VMEM,
        compiler_params=PARAMS,
        name="finish",
    )(lengths, cand_user.reshape(rows, 1), totals, gates, out_weight)
    terms = lax.all_to_all(terms, "head", 0, 0, tiled=True)
    return (cand_rows.astype(jnp.float32) + jnp.sum(terms, axis=0)).astype(jnp.bfloat16)


def solution(mesh):
    return jax.shard_map(
        local,
        mesh=mesh,
        in_specs=(
            P(("user", "seq"), "head"),
            P(None, None, "head"),
            P("head", None),
            P("user", "seq", "head"),
            P("user", "seq", "head"),
            P("user"),
            P(("user", "seq")),
        ),
        out_specs=P(("user", "seq"), "head"),
        check_vma=False,
    )
```

```python
import functools

import jax
import jax.numpy as jnp
from jax import lax
from jax.experimental import pallas as pl
from jax.experimental.pallas import tpu as pltpu
from jax.sharding import PartitionSpec as P

HEAD_DIM = 64
USERS = 2
VMEM = pl.BlockSpec(memory_space=pltpu.VMEM)
SMEM = pl.BlockSpec(memory_space=pltpu.SMEM)
PARAMS = pltpu.CompilerParams(vmem_limit_bytes=48 * 2**20)


SQUARE = (0, 4, 1, 5)


def role(place):
    return (place // 4) % 2, place % 2


def head_mask(shape, head):
    lane = lax.broadcasted_iota(jnp.int32, shape, len(shape) - 1)
    return (lane >= head * HEAD_DIM) & (lane < (head + 1) * HEAD_DIM)


def project_kernel(user_ref, cand_ref, weight_ref, query_ref, gate_ref):
    slices, rows, depth = cand_ref.shape
    width = weight_ref.shape[1] // 2
    total = jnp.zeros((rows, 2 * width), jnp.float32)
    for part in range(slices):
        total += jnp.dot(
            cand_ref[part],
            weight_ref[part * depth : (part + 1) * depth, :],
            preferred_element_type=jnp.float32,
        )
    projected = total / (1.0 + jnp.exp(-total))
    first = lax.broadcasted_iota(jnp.int32, (rows, rows), 0)
    second = lax.broadcasted_iota(jnp.int32, (rows, rows), 1)
    users = jnp.broadcast_to(user_ref[...], (rows, rows)).astype(jnp.bfloat16)
    before = jnp.dot(
        users, (first < second).astype(jnp.bfloat16), preferred_element_type=jnp.float32
    ).astype(jnp.int32)
    target = jnp.where(users > 0, rows // USERS + before, second - before)
    place = (target == first).astype(jnp.bfloat16)
    ordered = jnp.dot(
        place, projected.astype(jnp.bfloat16), preferred_element_type=jnp.float32
    )
    query = (ordered[:, :width] * (0.5 * HEAD_DIM**-0.5)).astype(jnp.bfloat16)
    _, block_rows, lanes = query_ref.shape
    for owner in range(query_ref.shape[0]):
        user, half = role(owner)
        query_ref[owner] = query[
            user * block_rows : (user + 1) * block_rows, half * lanes : (half + 1) * lanes
        ]
    gate_ref[...] = ordered[:, width:].astype(jnp.bfloat16)


def share_kernel(place_ref, key_ref, value_ref, *out_refs):
    lanes = out_refs[0].shape[2]
    for out_ref, offset in zip(out_refs, SQUARE):
        user, half = role(place_ref[0] ^ offset)
        here = pl.ds(pl.multiple_of(half * lanes, lanes), lanes)
        out_ref[0] = key_ref[user, :, here]
        out_ref[1] = value_ref[user, :, here]


def attend_kernel(
    rows_now, positions_now, place_ref, length_ref, query_ref, *rest
):
    history_refs, (out_ref, keys, masked) = rest[: len(SQUARE)], rest[len(SQUARE) :]
    blocks, block_rows, width = query_ref.shape
    heads = width // HEAD_DIM
    span = history_refs[0].shape[1]
    positions = span * len(SQUARE)
    step_blocks = rows_now // block_rows
    user, _ = role(place_ref[0])
    length = length_ref[user]
    for index, (offset, history_ref) in enumerate(zip(SQUARE, history_refs)):
        at = slice(index * span, (index + 1) * span)
        live = length - (place_ref[0] ^ offset) * span
        keys[:, at] = history_ref[0].T
        position = lax.broadcasted_iota(jnp.int32, (span, width), 0)
        value = history_ref[1]
        for head in range(heads):
            keep = (position < live) & head_mask((span, width), head)
            masked[head, at, :] = jnp.where(keep, value, jnp.zeros_like(value))

    def step(index, carry):
        here = pl.ds(index * step_blocks, step_blocks)
        query = query_ref[here].reshape(rows_now, width)
        total = jnp.zeros((rows_now, width), jnp.float32)
        for start in range(0, positions, positions_now):
            at = slice(start, start + positions_now)
            for head in range(heads):
                own = jnp.where(
                    head_mask((rows_now, width), head), query, jnp.zeros_like(query)
                )
                half = jnp.dot(own, keys[:, at], preferred_element_type=jnp.float32)
                weight = (half + half * jnp.tanh(half)).astype(jnp.bfloat16)
                total += jnp.dot(
                    weight, masked[head, at, :], preferred_element_type=jnp.float32
                )
        out_ref[here] = total.astype(jnp.bfloat16).reshape(step_blocks, block_rows, width)
        return carry

    lax.fori_loop(0, blocks // step_blocks, step, 0)


def finish_kernel(length_ref, user_ref, partial_ref, gate_ref, weight_ref, out_ref):
    rows, width = gate_ref.shape
    sums = {}
    for block in range(partial_ref.shape[0]):
        term = partial_ref[block].astype(jnp.float32)
        sums[role(block)] = sums[role(block)] + term if role(block) in sums else term
    total = jnp.concatenate(
        [jnp.concatenate([sums[user, half] for half in range(2)], axis=1) for user in range(USERS)],
        axis=0,
    )
    row = lax.broadcasted_iota(jnp.int32, (rows, width), 0)
    length = jnp.where(row < rows // USERS, length_ref[0], length_ref[1]).astype(jnp.float32)
    attn = total / length
    square = attn * attn
    mean = jnp.zeros((rows, width), jnp.float32)
    for head in range(width // HEAD_DIM):
        mask = head_mask((rows, width), head)
        summed = jnp.sum(jnp.where(mask, square, 0.0), axis=1, keepdims=True)
        mean = jnp.where(mask, summed * (1.0 / HEAD_DIM), mean)
    normed = attn * lax.rsqrt(mean + 1e-06)
    gated = (normed * gate_ref[...].astype(jnp.float32)).astype(jnp.bfloat16)
    first = lax.broadcasted_iota(jnp.int32, (rows, rows), 0)
    second = lax.broadcasted_iota(jnp.int32, (rows, rows), 1)
    users = jnp.broadcast_to(user_ref[...], (rows, rows)).astype(jnp.bfloat16)
    before = jnp.dot(
        (second < first).astype(jnp.bfloat16), users, preferred_element_type=jnp.float32
    ).astype(jnp.int32)
    target = jnp.where(users > 0, rows // USERS + before, first - before)
    back = (target == second).astype(jnp.bfloat16)
    gated = jnp.dot(back, gated, preferred_element_type=jnp.float32).astype(jnp.bfloat16)
    for part in range(out_ref.shape[0]):
        out_ref[part] = jnp.dot(
            gated,
            weight_ref[:, part * width : (part + 1) * width],
            preferred_element_type=jnp.float32,
        )


def local(cand_rows, qu_weight, out_weight, keys, values, lengths, cand_user):
    rows, depth = cand_rows.shape
    width = qu_weight.shape[2]
    positions = keys.shape[1]
    groups = lax.axis_size("head")
    owners = lax.axis_size("seq")
    place = jnp.reshape(lax.axis_index("seq"), (1,)).astype(jnp.int32)
    block_rows, lanes = rows // USERS, width // 2

    shares = pl.pallas_call(
        share_kernel,
        out_shape=[jax.ShapeDtypeStruct((2, positions, lanes), jnp.bfloat16) for _ in SQUARE],
        in_specs=[SMEM, VMEM, VMEM],
        out_specs=[VMEM for _ in SQUARE],
        compiler_params=PARAMS,
        name="share",
    )(place, keys, values)
    history = [
        lax.ppermute(share, "seq", [(s, s ^ offset) for s in range(owners)]) if offset else share
        for share, offset in zip(shares, SQUARE)
    ]

    copies = jnp.broadcast_to(cand_rows[None], (groups, rows, depth))
    cand_parts = lax.all_to_all(copies, "head", 0, 0, tiled=True)
    queries, gates = pl.pallas_call(
        project_kernel,
        out_shape=(
            jax.ShapeDtypeStruct((owners, block_rows, lanes), jnp.bfloat16),
            jax.ShapeDtypeStruct((rows, width), jnp.bfloat16),
        ),
        in_specs=[VMEM] * 3,
        out_specs=(VMEM, VMEM),
        compiler_params=PARAMS,
        name="project",
    )(
        cand_user.reshape(1, rows),
        cand_parts,
        qu_weight.reshape(qu_weight.shape[0], 2 * width),
    )
    queries = lax.all_to_all(queries, "seq", 0, 0, tiled=True)
    totals = pl.pallas_call(
        functools.partial(attend_kernel, 1024, 256),
        out_shape=jax.ShapeDtypeStruct((owners, block_rows, lanes), jnp.bfloat16),
        in_specs=[SMEM] * 2 + [VMEM] * (1 + len(SQUARE)),
        out_specs=VMEM,
        scratch_shapes=[
            pltpu.VMEM((lanes, len(SQUARE) * positions), jnp.bfloat16),
            pltpu.VMEM((lanes // HEAD_DIM, len(SQUARE) * positions, lanes), jnp.bfloat16),
        ],
        compiler_params=PARAMS,
        name="attend",
    )(place, lengths, queries, *history)
    totals = lax.all_to_all(totals, "seq", 0, 0, tiled=True)
    terms = pl.pallas_call(
        finish_kernel,
        out_shape=jax.ShapeDtypeStruct((groups, rows, depth), jnp.float32),
        in_specs=[SMEM] + [VMEM] * 4,
        out_specs=VMEM,
        compiler_params=PARAMS,
        name="finish",
    )(lengths, cand_user.reshape(rows, 1), totals, gates, out_weight)
    terms = lax.all_to_all(terms, "head", 0, 0, tiled=True)
    return (cand_rows.astype(jnp.float32) + jnp.sum(terms, axis=0)).astype(jnp.bfloat16)


def solution(mesh):
    return jax.shard_map(
        local,
        mesh=mesh,
        in_specs=(
            P(("user", "seq"), "head"),
            P(None, None, "head"),
            P("head", None),
            P("user", "seq", "head"),
            P("user", "seq", "head"),
            P("user"),
            P(("user", "seq")),
        ),
        out_specs=P(("user", "seq"), "head"),
        check_vma=False,
    )
```

```python
import functools

import jax
import jax.numpy as jnp
from jax import lax
from jax.experimental import pallas as pl
from jax.experimental.pallas import tpu as pltpu
from jax.sharding import PartitionSpec as P

HEAD_DIM = 64
USERS = 2
VMEM = pl.BlockSpec(memory_space=pltpu.VMEM)
SMEM = pl.BlockSpec(memory_space=pltpu.SMEM)
HBM = pl.BlockSpec(memory_space=pltpu.HBM)
PARAMS = pltpu.CompilerParams(vmem_limit_bytes=48 * 2**20)


SQUARE = (0, 4, 1, 5)


def role(place):
    return (place // 4) % 2, place % 2


def head_mask(shape, head):
    lane = lax.broadcasted_iota(jnp.int32, shape, len(shape) - 1)
    return (lane >= head * HEAD_DIM) & (lane < (head + 1) * HEAD_DIM)


def orders_of(users, rows):
    first = lax.broadcasted_iota(jnp.int32, (rows, rows), 0)
    second = lax.broadcasted_iota(jnp.int32, (rows, rows), 1)
    users = jnp.broadcast_to(users, (rows, rows))
    before = jnp.dot(
        users.astype(jnp.bfloat16),
        (first < second).astype(jnp.bfloat16),
        preferred_element_type=jnp.float32,
    ).astype(jnp.int32)
    target = jnp.where(users > 0, rows // USERS + before, second - before)
    order = (target == first).astype(jnp.float32)
    return order.astype(jnp.bfloat16), order.T.astype(jnp.bfloat16)


def project_kernel(place_ref, cand_ref, weight_ref, query_ref, gate_ref):
    slices, rows, depth = cand_ref.shape
    width = weight_ref.shape[1] // 2
    total = jnp.zeros((rows, 2 * width), jnp.float32)
    for part in range(slices):
        total += jnp.dot(
            cand_ref[part],
            weight_ref[part * depth : (part + 1) * depth, :],
            preferred_element_type=jnp.float32,
        )
    projected = total / (1.0 + jnp.exp(-total))
    ordered = jnp.dot(
        place_ref[...], projected.astype(jnp.bfloat16), preferred_element_type=jnp.float32
    )
    query = (ordered[:, :width] * (0.5 * HEAD_DIM**-0.5)).astype(jnp.bfloat16)
    _, block_rows, lanes = query_ref.shape
    for owner in range(query_ref.shape[0]):
        user, half = role(owner)
        query_ref[owner] = query[
            user * block_rows : (user + 1) * block_rows, half * lanes : (half + 1) * lanes
        ]
    gate_ref[...] = ordered[:, width:].astype(jnp.bfloat16)


def share_kernel(
    place_ref, user_ref, cand_ref, key_ref, value_ref, *rest
):
    out_refs, (copy_ref, order_ref, back_ref, sems) = rest[: len(SQUARE)], rest[len(SQUARE) :]
    lanes = out_refs[0].shape[2]
    copies = []
    for index, (out_ref, offset) in enumerate(zip(out_refs, SQUARE)):
        user, half = role(place_ref[0] ^ offset)
        here = pl.ds(pl.multiple_of(half * lanes, lanes), lanes)
        for kind, history_ref in enumerate((key_ref, value_ref)):
            copies.append(
                pltpu.make_async_copy(
                    history_ref.at[user, :, here], out_ref.at[kind], sems.at[index, kind]
                )
            )
    for copy in copies:
        copy.start()
    cand = cand_ref[...]
    for group in range(copy_ref.shape[0]):
        copy_ref[group] = cand
    order, back = orders_of(user_ref[...], cand.shape[0])
    order_ref[...] = order
    back_ref[...] = back
    for copy in copies:
        copy.wait()


def attend_kernel(
    rows_now, positions_now, place_ref, length_ref, query_ref, *rest
):
    history_refs, (out_ref, keys, masked) = rest[: len(SQUARE)], rest[len(SQUARE) :]
    blocks, block_rows, width = query_ref.shape
    heads = width // HEAD_DIM
    span = history_refs[0].shape[1]
    positions = span * len(SQUARE)
    step_blocks = rows_now // block_rows
    user, _ = role(place_ref[0])
    length = length_ref[user]
    for index, (offset, history_ref) in enumerate(zip(SQUARE, history_refs)):
        at = slice(index * span, (index + 1) * span)
        live = length - (place_ref[0] ^ offset) * span
        keys[:, at] = history_ref[0].T
        position = lax.broadcasted_iota(jnp.int32, (span, width), 0)
        value = history_ref[1]
        for head in range(heads):
            keep = (position < live) & head_mask((span, width), head)
            masked[head, at, :] = jnp.where(keep, value, jnp.zeros_like(value))

    def step(index, carry):
        here = pl.ds(index * step_blocks, step_blocks)
        query = query_ref[here].reshape(rows_now, width)
        total = jnp.zeros((rows_now, width), jnp.float32)
        for start in range(0, positions, positions_now):
            at = slice(start, start + positions_now)
            for head in range(heads):
                own = jnp.where(
                    head_mask((rows_now, width), head), query, jnp.zeros_like(query)
                )
                half = jnp.dot(own, keys[:, at], preferred_element_type=jnp.float32)
                weight = (half + half * jnp.tanh(half)).astype(jnp.bfloat16)
                total += jnp.dot(
                    weight, masked[head, at, :], preferred_element_type=jnp.float32
                )
        out_ref[here] = total.astype(jnp.bfloat16).reshape(step_blocks, block_rows, width)
        return carry

    lax.fori_loop(0, blocks // step_blocks, step, 0)


def finish_kernel(length_ref, back_ref, partial_ref, gate_ref, weight_ref, out_ref):
    rows, width = gate_ref.shape
    sums = {}
    for block in range(partial_ref.shape[0]):
        term = partial_ref[block].astype(jnp.float32)
        sums[role(block)] = sums[role(block)] + term if role(block) in sums else term
    total = jnp.concatenate(
        [jnp.concatenate([sums[user, half] for half in range(2)], axis=1) for user in range(USERS)],
        axis=0,
    )
    row = lax.broadcasted_iota(jnp.int32, (rows, width), 0)
    length = jnp.where(row < rows // USERS, length_ref[0], length_ref[1]).astype(jnp.float32)
    attn = total / length
    square = attn * attn
    mean = jnp.zeros((rows, width), jnp.float32)
    for head in range(width // HEAD_DIM):
        mask = head_mask((rows, width), head)
        summed = jnp.sum(jnp.where(mask, square, 0.0), axis=1, keepdims=True)
        mean = jnp.where(mask, summed * (1.0 / HEAD_DIM), mean)
    normed = attn * lax.rsqrt(mean + 1e-06)
    gated = (normed * gate_ref[...]).astype(jnp.bfloat16)
    gated = jnp.dot(back_ref[...], gated, preferred_element_type=jnp.float32).astype(jnp.bfloat16)
    for part in range(out_ref.shape[0]):
        out_ref[part] = jnp.dot(
            gated,
            weight_ref[:, part * width : (part + 1) * width],
            preferred_element_type=jnp.float32,
        ).astype(out_ref.dtype)


def add_kernel(cand_ref, term_ref, out_ref):
    total = cand_ref[...]
    for group in range(term_ref.shape[0]):
        total += term_ref[group].astype(jnp.float32)
    out_ref[...] = total.astype(out_ref.dtype)


def local(cand_rows, qu_weight, out_weight, keys, values, lengths, cand_user):
    rows, depth = cand_rows.shape
    width = qu_weight.shape[2]
    positions = keys.shape[1]
    groups = lax.axis_size("head")
    owners = lax.axis_size("seq")
    place = jnp.reshape(lax.axis_index("seq"), (1,)).astype(jnp.int32)
    block_rows, lanes = rows // USERS, width // 2

    *shares, copies, order, back = pl.pallas_call(
        share_kernel,
        out_shape=[jax.ShapeDtypeStruct((2, positions, lanes), jnp.bfloat16) for _ in SQUARE]
        + [
            jax.ShapeDtypeStruct((groups, rows, depth), jnp.bfloat16),
            jax.ShapeDtypeStruct((rows, rows), jnp.bfloat16),
            jax.ShapeDtypeStruct((rows, rows), jnp.bfloat16),
        ],
        in_specs=[SMEM, VMEM, VMEM, HBM, HBM],
        out_specs=[HBM] * len(SQUARE) + [VMEM] * 3,
        scratch_shapes=[pltpu.SemaphoreType.DMA((len(SQUARE), 2))],
        compiler_params=pltpu.CompilerParams(vmem_limit_bytes=60 * 2**20),
        name="share",
    )(place, cand_user.reshape(1, rows), cand_rows, keys, values)
    history = [
        lax.ppermute(share, "seq", [(s, s ^ offset) for s in range(owners)]) if offset else share
        for share, offset in zip(shares, SQUARE)
    ]

    cand_parts = lax.all_to_all(copies, "head", 0, 0, tiled=True)
    queries, gates = pl.pallas_call(
        project_kernel,
        out_shape=(
            jax.ShapeDtypeStruct((owners, block_rows, lanes), jnp.bfloat16),
            jax.ShapeDtypeStruct((rows, width), jnp.bfloat16),
        ),
        in_specs=[VMEM] * 3,
        out_specs=(VMEM, VMEM),
        compiler_params=PARAMS,
        name="project",
    )(
        order,
        cand_parts,
        qu_weight.reshape(qu_weight.shape[0], 2 * width),
    )
    queries = lax.all_to_all(queries, "seq", 0, 0, tiled=True)
    totals = pl.pallas_call(
        functools.partial(attend_kernel, 1024, 256),
        out_shape=jax.ShapeDtypeStruct((owners, block_rows, lanes), jnp.bfloat16),
        in_specs=[SMEM] * 2 + [VMEM] * (1 + len(SQUARE)),
        out_specs=VMEM,
        scratch_shapes=[
            pltpu.VMEM((lanes, len(SQUARE) * positions), jnp.bfloat16),
            pltpu.VMEM((lanes // HEAD_DIM, len(SQUARE) * positions, lanes), jnp.bfloat16),
        ],
        compiler_params=PARAMS,
        name="attend",
    )(place, lengths, queries, *history)
    totals = lax.all_to_all(totals, "seq", 0, 0, tiled=True)
    terms = pl.pallas_call(
        finish_kernel,
        out_shape=jax.ShapeDtypeStruct((groups, rows, depth), jnp.bfloat16),
        in_specs=[SMEM] + [VMEM] * 4,
        out_specs=VMEM,
        compiler_params=PARAMS,
        name="finish",
    )(lengths, back, totals, gates.astype(jnp.float32), out_weight)
    terms = lax.all_to_all(terms, "head", 0, 0, tiled=True)
    return pl.pallas_call(
        add_kernel,
        out_shape=jax.ShapeDtypeStruct((rows, depth), cand_rows.dtype),
        in_specs=[VMEM, VMEM],
        out_specs=VMEM,
        compiler_params=PARAMS,
        name="add",
    )(cand_rows.astype(jnp.float32), terms)


def solution(mesh):
    return jax.shard_map(
        local,
        mesh=mesh,
        in_specs=(
            P(("user", "seq"), "head"),
            P(None, None, "head"),
            P("head", None),
            P("user", "seq", "head"),
            P("user", "seq", "head"),
            P("user"),
            P(("user", "seq")),
        ),
        out_specs=P(("user", "seq"), "head"),
        check_vma=False,
    )
```

```python
import functools

import jax
import jax.numpy as jnp
from jax import lax
from jax.experimental import pallas as pl
from jax.experimental.pallas import tpu as pltpu
from jax.sharding import PartitionSpec as P

HEAD_DIM = 64
USERS = 2
VMEM = pl.BlockSpec(memory_space=pltpu.VMEM)
SMEM = pl.BlockSpec(memory_space=pltpu.SMEM)
HBM = pl.BlockSpec(memory_space=pltpu.HBM)
PARAMS = pltpu.CompilerParams(vmem_limit_bytes=48 * 2**20)


SOURCES = 4


def role(place):
    return (place // 4) % 2, (place // 8 + place) % 2


def source(place, index, owners):
    if index == 0:
        return place
    if index == 3:
        return place + 1 - 2 * (place % 2)
    step = 4 - 8 * ((place // 4) % 2)
    return (place + (step if index == 1 else -step) + owners) % owners


def head_mask(shape, head):
    lane = lax.broadcasted_iota(jnp.int32, shape, len(shape) - 1)
    return (lane >= head * HEAD_DIM) & (lane < (head + 1) * HEAD_DIM)


def orders_of(users, rows):
    first = lax.broadcasted_iota(jnp.int32, (rows, rows), 0)
    second = lax.broadcasted_iota(jnp.int32, (rows, rows), 1)
    users = jnp.broadcast_to(users, (rows, rows))
    before = jnp.dot(
        users.astype(jnp.bfloat16),
        (first < second).astype(jnp.bfloat16),
        preferred_element_type=jnp.float32,
    ).astype(jnp.int32)
    target = jnp.where(users > 0, rows // USERS + before, second - before)
    order = (target == first).astype(jnp.float32)
    return order.astype(jnp.bfloat16), order.T.astype(jnp.bfloat16)


def project_kernel(place_ref, cand_ref, weight_ref, query_ref, gate_ref):
    slices, rows, depth = cand_ref.shape
    width = weight_ref.shape[1] // 2
    total = jnp.zeros((rows, 2 * width), jnp.float32)
    for part in range(slices):
        total += jnp.dot(
            cand_ref[part],
            weight_ref[part * depth : (part + 1) * depth, :],
            preferred_element_type=jnp.float32,
        )
    projected = total / (1.0 + jnp.exp(-total))
    ordered = jnp.dot(
        place_ref[...], projected.astype(jnp.bfloat16), preferred_element_type=jnp.float32
    )
    query = (ordered[:, :width] * (0.5 * HEAD_DIM**-0.5)).astype(jnp.bfloat16)
    _, block_rows, lanes = query_ref.shape
    for owner in range(query_ref.shape[0]):
        user, half = role(owner)
        query_ref[owner] = query[
            user * block_rows : (user + 1) * block_rows, half * lanes : (half + 1) * lanes
        ]
    gate_ref[...] = ordered[:, width:].astype(jnp.bfloat16)


def share_kernel(
    owners, place_ref, user_ref, cand_ref, key_ref, value_ref, *rest
):
    out_refs, (copy_ref, order_ref, back_ref, sems) = rest[:SOURCES], rest[SOURCES:]
    lanes = out_refs[0].shape[2]
    copies = []
    for index, out_ref in enumerate(out_refs):
        user, half = role(source(place_ref[0], index, owners))
        here = pl.ds(pl.multiple_of(half * lanes, lanes), lanes)
        for kind, history_ref in enumerate((key_ref, value_ref)):
            copies.append(
                pltpu.make_async_copy(
                    history_ref.at[user, :, here], out_ref.at[kind], sems.at[index, kind]
                )
            )
    for copy in copies:
        copy.start()
    cand = cand_ref[...]
    for group in range(copy_ref.shape[0]):
        copy_ref[group] = cand
    order, back = orders_of(user_ref[...], cand.shape[0])
    order_ref[...] = order
    back_ref[...] = back
    for copy in copies:
        copy.wait()


def attend_kernel(
    rows_now, positions_now, place_ref, length_ref, query_ref, *rest
):
    history_refs, (out_ref, keys, masked) = rest[:SOURCES], rest[SOURCES:]
    blocks, block_rows, width = query_ref.shape
    heads = width // HEAD_DIM
    span = history_refs[0].shape[1]
    positions = span * SOURCES
    step_blocks = rows_now // block_rows
    user, _ = role(place_ref[0])
    length = length_ref[user]
    for index, history_ref in enumerate(history_refs):
        at = slice(index * span, (index + 1) * span)
        live = length - source(place_ref[0], index, blocks) * span
        keys[:, at] = history_ref[0].T
        position = lax.broadcasted_iota(jnp.int32, (span, width), 0)
        value = history_ref[1]
        for head in range(heads):
            keep = (position < live) & head_mask((span, width), head)
            masked[head, at, :] = jnp.where(keep, value, jnp.zeros_like(value))

    def step(index, carry):
        here = pl.ds(index * step_blocks, step_blocks)
        query = query_ref[here].reshape(rows_now, width)
        total = jnp.zeros((rows_now, width), jnp.float32)
        for start in range(0, positions, positions_now):
            at = slice(start, start + positions_now)
            for head in range(heads):
                own = jnp.where(
                    head_mask((rows_now, width), head), query, jnp.zeros_like(query)
                )
                half = jnp.dot(own, keys[:, at], preferred_element_type=jnp.float32)
                weight = (half + half * jnp.tanh(half)).astype(jnp.bfloat16)
                total += jnp.dot(
                    weight, masked[head, at, :], preferred_element_type=jnp.float32
                )
        out_ref[here] = total.astype(jnp.bfloat16).reshape(step_blocks, block_rows, width)
        return carry

    lax.fori_loop(0, blocks // step_blocks, step, 0)


def finish_kernel(length_ref, back_ref, partial_ref, gate_ref, weight_ref, out_ref):
    rows, width = gate_ref.shape
    sums = {}
    for block in range(partial_ref.shape[0]):
        term = partial_ref[block].astype(jnp.float32)
        sums[role(block)] = sums[role(block)] + term if role(block) in sums else term
    total = jnp.concatenate(
        [jnp.concatenate([sums[user, half] for half in range(2)], axis=1) for user in range(USERS)],
        axis=0,
    )
    row = lax.broadcasted_iota(jnp.int32, (rows, width), 0)
    length = jnp.where(row < rows // USERS, length_ref[0], length_ref[1]).astype(jnp.float32)
    attn = total / length
    square = attn * attn
    mean = jnp.zeros((rows, width), jnp.float32)
    for head in range(width // HEAD_DIM):
        mask = head_mask((rows, width), head)
        summed = jnp.sum(jnp.where(mask, square, 0.0), axis=1, keepdims=True)
        mean = jnp.where(mask, summed * (1.0 / HEAD_DIM), mean)
    normed = attn * lax.rsqrt(mean + 1e-06)
    gated = (normed * gate_ref[...]).astype(jnp.bfloat16)
    gated = jnp.dot(back_ref[...], gated, preferred_element_type=jnp.float32).astype(jnp.bfloat16)
    for part in range(out_ref.shape[0]):
        out_ref[part] = jnp.dot(
            gated,
            weight_ref[:, part * width : (part + 1) * width],
            preferred_element_type=jnp.float32,
        ).astype(out_ref.dtype)


def add_kernel(cand_ref, term_ref, out_ref):
    total = cand_ref[...]
    for group in range(term_ref.shape[0]):
        total += term_ref[group].astype(jnp.float32)
    out_ref[...] = total.astype(out_ref.dtype)


def local(cand_rows, qu_weight, out_weight, keys, values, lengths, cand_user):
    rows, depth = cand_rows.shape
    width = qu_weight.shape[2]
    positions = keys.shape[1]
    groups = lax.axis_size("head")
    owners = lax.axis_size("seq")
    place = jnp.reshape(lax.axis_index("seq"), (1,)).astype(jnp.int32)
    block_rows, lanes = rows // USERS, width // 2

    *shares, copies, order, back = pl.pallas_call(
        functools.partial(share_kernel, owners),
        out_shape=[jax.ShapeDtypeStruct((2, positions, lanes), jnp.bfloat16)] * SOURCES
        + [
            jax.ShapeDtypeStruct((groups, rows, depth), jnp.bfloat16),
            jax.ShapeDtypeStruct((rows, rows), jnp.bfloat16),
            jax.ShapeDtypeStruct((rows, rows), jnp.bfloat16),
        ],
        in_specs=[SMEM, VMEM, VMEM, HBM, HBM],
        out_specs=[VMEM] * (SOURCES + 3),
        scratch_shapes=[pltpu.SemaphoreType.DMA((SOURCES, 2))],
        compiler_params=pltpu.CompilerParams(vmem_limit_bytes=60 * 2**20),
        name="share",
    )(place, cand_user.reshape(1, rows), cand_rows, keys, values)
    history = shares[:1] + [
        lax.ppermute(shares[index], "seq", [(s, source(s, index, owners)) for s in range(owners)])
        for index in range(1, SOURCES)
    ]

    cand_parts = lax.all_to_all(copies, "head", 0, 0, tiled=True)
    queries, gates = pl.pallas_call(
        project_kernel,
        out_shape=(
            jax.ShapeDtypeStruct((owners, block_rows, lanes), jnp.bfloat16),
            jax.ShapeDtypeStruct((rows, width), jnp.bfloat16),
        ),
        in_specs=[VMEM] * 3,
        out_specs=(VMEM, VMEM),
        compiler_params=PARAMS,
        name="project",
    )(
        order,
        cand_parts,
        qu_weight.reshape(qu_weight.shape[0], 2 * width),
    )
    queries = lax.all_to_all(queries, "seq", 0, 0, tiled=True)
    totals = pl.pallas_call(
        functools.partial(attend_kernel, 1024, 256),
        out_shape=jax.ShapeDtypeStruct((owners, block_rows, lanes), jnp.bfloat16),
        in_specs=[SMEM] * 2 + [VMEM] * (1 + SOURCES),
        out_specs=VMEM,
        scratch_shapes=[
            pltpu.VMEM((lanes, SOURCES * positions), jnp.bfloat16),
            pltpu.VMEM((lanes // HEAD_DIM, SOURCES * positions, lanes), jnp.bfloat16),
        ],
        compiler_params=PARAMS,
        name="attend",
    )(place, lengths, queries, *history)
    totals = lax.all_to_all(totals, "seq", 0, 0, tiled=True)
    terms = pl.pallas_call(
        finish_kernel,
        out_shape=jax.ShapeDtypeStruct((groups, rows, depth), jnp.bfloat16),
        in_specs=[SMEM] + [VMEM] * 4,
        out_specs=VMEM,
        compiler_params=PARAMS,
        name="finish",
    )(lengths, back, totals, gates.astype(jnp.float32), out_weight)
    terms = lax.all_to_all(terms, "head", 0, 0, tiled=True)
    return pl.pallas_call(
        add_kernel,
        out_shape=jax.ShapeDtypeStruct((rows, depth), cand_rows.dtype),
        in_specs=[VMEM, VMEM],
        out_specs=VMEM,
        compiler_params=PARAMS,
        name="add",
    )(cand_rows.astype(jnp.float32), terms)


def solution(mesh):
    return jax.shard_map(
        local,
        mesh=mesh,
        in_specs=(
            P(("user", "seq"), "head"),
            P(None, None, "head"),
            P("head", None),
            P("user", "seq", "head"),
            P("user", "seq", "head"),
            P("user"),
            P(("user", "seq")),
        ),
        out_specs=P(("user", "seq"), "head"),
        check_vma=False,
    )
```

```python
import functools

import jax
import jax.numpy as jnp
from jax import lax
from jax.experimental import pallas as pl
from jax.experimental.pallas import tpu as pltpu
from jax.sharding import PartitionSpec as P

HEAD_DIM = 64
USERS = 2
VMEM = pl.BlockSpec(memory_space=pltpu.VMEM)
SMEM = pl.BlockSpec(memory_space=pltpu.SMEM)
HBM = pl.BlockSpec(memory_space=pltpu.HBM)
PARAMS = pltpu.CompilerParams(vmem_limit_bytes=16 * 2**20)
ATTEND_PARAMS = pltpu.CompilerParams(vmem_limit_bytes=32 * 2**20)


SOURCES = 4


def role(place):
    return (place // 4) % 2, (place // 8 + place) % 2


def source(place, index, owners):
    if index == 0:
        return place
    if index == 3:
        return place + 1 - 2 * (place % 2)
    step = 4 - 8 * ((place // 4) % 2)
    return (place + (step if index == 1 else -step) + owners) % owners


def head_mask(shape, head):
    lane = lax.broadcasted_iota(jnp.int32, shape, len(shape) - 1)
    return (lane >= head * HEAD_DIM) & (lane < (head + 1) * HEAD_DIM)


def orders_of(users, rows):
    first = lax.broadcasted_iota(jnp.int32, (rows, rows), 0)
    second = lax.broadcasted_iota(jnp.int32, (rows, rows), 1)
    users = jnp.broadcast_to(users, (rows, rows))
    before = jnp.dot(
        users.astype(jnp.bfloat16),
        (first < second).astype(jnp.bfloat16),
        preferred_element_type=jnp.float32,
    ).astype(jnp.int32)
    target = jnp.where(users > 0, rows // USERS + before, second - before)
    order = (target == first).astype(jnp.float32)
    return order.astype(jnp.bfloat16), order.T.astype(jnp.bfloat16)


def project_kernel(place_ref, cand_ref, weight_ref, query_ref, gate_ref):
    slices, rows, depth = cand_ref.shape
    width = weight_ref.shape[1] // 2
    total = jnp.zeros((rows, 2 * width), jnp.float32)
    for part in range(slices):
        total += jnp.dot(
            cand_ref[part],
            weight_ref[part * depth : (part + 1) * depth, :],
            preferred_element_type=jnp.float32,
        )
    projected = total / (1.0 + jnp.exp(-total))
    ordered = jnp.dot(
        place_ref[...], projected.astype(jnp.bfloat16), preferred_element_type=jnp.float32
    )
    query = (ordered[:, :width] * (0.5 * HEAD_DIM**-0.5)).astype(jnp.bfloat16)
    _, block_rows, lanes = query_ref.shape
    for owner in range(query_ref.shape[0]):
        user, half = role(owner)
        query_ref[owner] = query[
            user * block_rows : (user + 1) * block_rows, half * lanes : (half + 1) * lanes
        ]
    gate_ref[...] = ordered[:, width:].astype(jnp.bfloat16)


def share_kernel(
    owners, place_ref, user_ref, cand_ref, weight_ref, key_ref, value_ref, *rest
):
    out_refs, rest = rest[:SOURCES], rest[SOURCES:]
    copy_ref, keep_ref, order_ref, back_ref, held_ref, users, parts, sems, own_sems = rest
    lanes = out_refs[0].shape[2]
    first = [
        pltpu.make_async_copy(cand_ref, keep_ref, own_sems.at[0]),
        pltpu.make_async_copy(user_ref, users, own_sems.at[1]),
    ]
    into = []
    for index in range(SOURCES):
        user, half = role(source(place_ref[0], index, owners))
        here = pl.ds(pl.multiple_of(half * lanes, lanes), lanes)
        for kind, history_ref in enumerate((key_ref, value_ref)):
            into.append(
                pltpu.make_async_copy(
                    history_ref.at[user, :, here], parts.at[index, kind], sems.at[index, kind]
                )
            )
    last = pltpu.make_async_copy(weight_ref, held_ref, own_sems.at[2])
    for copy in first + into + [last]:
        copy.start()
    for copy in first:
        copy.wait()
    cand = keep_ref[...]
    for group in range(copy_ref.shape[0]):
        copy_ref[group] = cand
    order, back = orders_of(users[...], cand.shape[0])
    order_ref[...] = order
    back_ref[...] = back
    out = []
    for index, out_ref in enumerate(out_refs):
        for kind in range(2):
            into[2 * index + kind].wait()
            out.append(
                pltpu.make_async_copy(
                    parts.at[index, kind], out_ref.at[kind], sems.at[index, kind]
                )
            )
            out[-1].start()
    last.wait()
    for copy in out:
        copy.wait()


def prepare_kernel(owners, place_ref, length_ref, *rest):
    history_refs, (key_ref, value_ref) = rest[:SOURCES], rest[SOURCES:]
    _, span, width = history_refs[0].shape
    user, _ = role(place_ref[0])
    length = length_ref[user]
    position = lax.broadcasted_iota(jnp.int32, (span, width), 0)
    for index, history_ref in enumerate(history_refs):
        at = slice(index * span, (index + 1) * span)
        live = length - source(place_ref[0], index, owners) * span
        key_ref[:, at] = history_ref[0].T
        value = history_ref[1]
        for head in range(width // HEAD_DIM):
            keep = (position < live) & head_mask((span, width), head)
            value_ref[head, at, :] = jnp.where(keep, value, jnp.zeros_like(value))


def attend_kernel(rows_now, positions_now, query_ref, keys, masked, out_ref):
    blocks, block_rows, width = query_ref.shape
    heads, positions, _ = masked.shape
    step_blocks = rows_now // block_rows

    def step(index, carry):
        here = pl.ds(index * step_blocks, step_blocks)
        query = query_ref[here].reshape(rows_now, width)
        total = jnp.zeros((rows_now, width), jnp.float32)
        for start in range(0, positions, positions_now):
            at = slice(start, start + positions_now)
            for head in range(heads):
                own = jnp.where(
                    head_mask((rows_now, width), head), query, jnp.zeros_like(query)
                )
                half = jnp.dot(own, keys[:, at], preferred_element_type=jnp.float32)
                weight = (half + half * jnp.tanh(half)).astype(jnp.bfloat16)
                total += jnp.dot(
                    weight, masked[head, at, :], preferred_element_type=jnp.float32
                )
        out_ref[here] = total.astype(jnp.bfloat16).reshape(step_blocks, block_rows, width)
        return carry

    lax.fori_loop(0, blocks // step_blocks, step, 0)


def finish_kernel(
    length_ref, back_ref, partial_ref, gate_ref, source_ref, out_ref, weight_ref, sem
):
    rows, width = gate_ref.shape
    fetch = pltpu.make_async_copy(source_ref, weight_ref, sem)
    fetch.start()
    sums = {}
    for block in range(partial_ref.shape[0]):
        term = partial_ref[block].astype(jnp.float32)
        sums[role(block)] = sums[role(block)] + term if role(block) in sums else term
    total = jnp.concatenate(
        [jnp.concatenate([sums[user, half] for half in range(2)], axis=1) for user in range(USERS)],
        axis=0,
    )
    row = lax.broadcasted_iota(jnp.int32, (rows, width), 0)
    length = jnp.where(row < rows // USERS, length_ref[0], length_ref[1]).astype(jnp.float32)
    attn = total / length
    square = attn * attn
    mean = jnp.zeros((rows, width), jnp.float32)
    for head in range(width // HEAD_DIM):
        mask = head_mask((rows, width), head)
        summed = jnp.sum(jnp.where(mask, square, 0.0), axis=1, keepdims=True)
        mean = jnp.where(mask, summed * (1.0 / HEAD_DIM), mean)
    normed = attn * lax.rsqrt(mean + 1e-06)
    gated = (normed * gate_ref[...]).astype(jnp.bfloat16)
    gated = jnp.dot(back_ref[...], gated, preferred_element_type=jnp.float32).astype(jnp.bfloat16)
    fetch.wait()
    for part in range(out_ref.shape[0]):
        out_ref[part] = jnp.dot(
            gated,
            weight_ref[:, part * width : (part + 1) * width],
            preferred_element_type=jnp.float32,
        ).astype(out_ref.dtype)


def add_kernel(cand_ref, term_ref, out_ref):
    total = cand_ref[...].astype(jnp.float32)
    for group in range(term_ref.shape[0]):
        total += term_ref[group].astype(jnp.float32)
    out_ref[...] = total.astype(out_ref.dtype)


def in_hbm(array):
    return pltpu.with_memory_space_constraint(array, pltpu.HBM)


def local(cand_rows, qu_weight, out_weight, keys, values, lengths, cand_user):
    rows, depth = cand_rows.shape
    width = qu_weight.shape[2]
    positions = keys.shape[1]
    groups = lax.axis_size("head")
    owners = lax.axis_size("seq")
    place = jnp.reshape(lax.axis_index("seq"), (1,)).astype(jnp.int32)
    block_rows, lanes = rows // USERS, width // 2

    *shares, copies, kept, order, back, weight = pl.pallas_call(
        functools.partial(share_kernel, owners),
        out_shape=[pltpu.HBM((2, positions, lanes), jnp.bfloat16)] * SOURCES
        + [
            jax.ShapeDtypeStruct((groups, rows, depth), jnp.bfloat16),
            pltpu.VMEM((rows, depth), jnp.bfloat16),
            pltpu.VMEM((rows, rows), jnp.bfloat16),
            pltpu.VMEM((rows, rows), jnp.bfloat16),
            pltpu.VMEM(qu_weight.shape, jnp.bfloat16),
        ],
        in_specs=[SMEM] + [HBM] * 5,
        out_specs=[HBM] * SOURCES + [VMEM] * 5,
        scratch_shapes=[
            pltpu.VMEM((1, rows), jnp.int32),
            pltpu.VMEM((SOURCES, 2, positions, lanes), jnp.bfloat16),
            pltpu.SemaphoreType.DMA((SOURCES, 2)),
            pltpu.SemaphoreType.DMA((3,)),
        ],
        compiler_params=PARAMS,
        name="share",
    )(place, *map(in_hbm, (cand_user.reshape(1, rows), cand_rows, qu_weight, keys, values)))
    history = shares[:1] + [
        lax.ppermute(shares[index], "seq", [(s, source(s, index, owners)) for s in range(owners)])
        for index in range(1, SOURCES)
    ]

    cand_parts = lax.all_to_all(copies, "head", 0, 0, tiled=True)
    queries, gates = pl.pallas_call(
        project_kernel,
        out_shape=(
            jax.ShapeDtypeStruct((owners, block_rows, lanes), jnp.bfloat16),
            jax.ShapeDtypeStruct((rows, width), jnp.bfloat16),
        ),
        in_specs=[VMEM] * 3,
        out_specs=(VMEM, VMEM),
        compiler_params=PARAMS,
        name="project",
    )(
        order,
        cand_parts,
        weight.reshape(qu_weight.shape[0], 2 * width),
    )
    queries = lax.all_to_all(queries, "seq", 0, 0, tiled=True)
    turned, masked = pl.pallas_call(
        functools.partial(prepare_kernel, owners),
        out_shape=(
            jax.ShapeDtypeStruct((lanes, SOURCES * positions), jnp.bfloat16),
            jax.ShapeDtypeStruct(
                (lanes // HEAD_DIM, SOURCES * positions, lanes), jnp.bfloat16
            ),
        ),
        in_specs=[SMEM] * 2 + [VMEM] * SOURCES,
        out_specs=(VMEM, VMEM),
        compiler_params=PARAMS,
        name="prepare",
    )(place, lengths, *map(in_hbm, history))
    totals = pl.pallas_call(
        functools.partial(attend_kernel, 1024, 256),
        out_shape=jax.ShapeDtypeStruct((owners, block_rows, lanes), jnp.bfloat16),
        in_specs=[VMEM] * 3,
        out_specs=VMEM,
        compiler_params=ATTEND_PARAMS,
        name="attend",
    )(queries, turned, masked)
    totals = lax.all_to_all(totals, "seq", 0, 0, tiled=True)
    terms = pl.pallas_call(
        finish_kernel,
        out_shape=jax.ShapeDtypeStruct((groups, rows, depth), jnp.bfloat16),
        in_specs=[SMEM] + [VMEM] * 3 + [HBM],
        out_specs=VMEM,
        scratch_shapes=[pltpu.VMEM(out_weight.shape, jnp.bfloat16), pltpu.SemaphoreType.DMA],
        compiler_params=PARAMS,
        name="finish",
    )(lengths, back, totals, gates.astype(jnp.float32), in_hbm(out_weight))
    terms = lax.all_to_all(terms, "head", 0, 0, tiled=True)
    return pl.pallas_call(
        add_kernel,
        out_shape=jax.ShapeDtypeStruct((rows, depth), cand_rows.dtype),
        in_specs=[VMEM, VMEM],
        out_specs=VMEM,
        compiler_params=PARAMS,
        name="add",
    )(kept, terms)


def solution(mesh):
    return jax.shard_map(
        local,
        mesh=mesh,
        in_specs=(
            P(("user", "seq"), "head"),
            P(None, None, "head"),
            P("head", None),
            P("user", "seq", "head"),
            P("user", "seq", "head"),
            P("user"),
            P(("user", "seq")),
        ),
        out_specs=P(("user", "seq"), "head"),
        check_vma=False,
    )
```

```python
import functools

import jax
import jax.numpy as jnp
from jax import lax
from jax.experimental import pallas as pl
from jax.experimental.pallas import tpu as pltpu
from jax.sharding import PartitionSpec as P

HEAD_DIM = 64
USERS = 2
VMEM = pl.BlockSpec(memory_space=pltpu.VMEM)
SMEM = pl.BlockSpec(memory_space=pltpu.SMEM)
HBM = pl.BlockSpec(memory_space=pltpu.HBM)
PARAMS = pltpu.CompilerParams(vmem_limit_bytes=16 * 2**20)
ATTEND_PARAMS = pltpu.CompilerParams(vmem_limit_bytes=32 * 2**20)


SOURCES = 4


def role(place):
    return (place // 4) % 2, (place // 8 + place) % 2


def source(place, index, owners):
    if index == 0:
        return place
    if index == 3:
        return place + 1 - 2 * (place % 2)
    step = 4 - 8 * ((place // 4) % 2)
    return (place + (step if index == 1 else -step) + owners) % owners


def head_mask(shape, head):
    lane = lax.broadcasted_iota(jnp.int32, shape, len(shape) - 1)
    return (lane >= head * HEAD_DIM) & (lane < (head + 1) * HEAD_DIM)


def orders_of(users, rows):
    first = lax.broadcasted_iota(jnp.int32, (rows, rows), 0)
    second = lax.broadcasted_iota(jnp.int32, (rows, rows), 1)
    users = jnp.broadcast_to(users, (rows, rows))
    before = jnp.dot(
        users.astype(jnp.bfloat16),
        (first < second).astype(jnp.bfloat16),
        preferred_element_type=jnp.float32,
    ).astype(jnp.int32)
    target = jnp.where(users > 0, rows // USERS + before, second - before)
    order = (target == first).astype(jnp.float32)
    return order.astype(jnp.bfloat16), order.T.astype(jnp.bfloat16)


def project_kernel(place_ref, cand_ref, weight_ref, query_ref, gate_ref):
    slices, rows, depth = cand_ref.shape
    width = weight_ref.shape[1] // 2
    total = jnp.zeros((rows, 2 * width), jnp.float32)
    for part in range(slices):
        total += jnp.dot(
            cand_ref[part],
            weight_ref[part * depth : (part + 1) * depth, :],
            preferred_element_type=jnp.float32,
        )
    projected = total / (1.0 + jnp.exp(-total))
    ordered = jnp.dot(
        place_ref[...], projected.astype(jnp.bfloat16), preferred_element_type=jnp.float32
    )
    query = (ordered[:, :width] * (0.5 * HEAD_DIM**-0.5)).astype(jnp.bfloat16)
    _, block_rows, lanes = query_ref.shape
    for owner in range(query_ref.shape[0]):
        user, half = role(owner)
        query_ref[owner] = query[
            user * block_rows : (user + 1) * block_rows, half * lanes : (half + 1) * lanes
        ]
    gate_ref[...] = ordered[:, width:].astype(jnp.bfloat16)


def share_kernel(
    owners, place_ref, user_ref, cand_ref, weight_ref, key_ref, value_ref, *rest
):
    out_refs, rest = rest[:SOURCES], rest[SOURCES:]
    copy_ref, keep_ref, order_ref, back_ref, held_ref, users, parts, sems, own_sems = rest
    lanes = out_refs[0].shape[2]
    first = [
        pltpu.make_async_copy(cand_ref, keep_ref, own_sems.at[0]),
        pltpu.make_async_copy(user_ref, users, own_sems.at[1]),
    ]
    into = []
    for index in range(SOURCES):
        user, half = role(source(place_ref[0], index, owners))
        here = pl.ds(pl.multiple_of(half * lanes, lanes), lanes)
        for kind, history_ref in enumerate((key_ref, value_ref)):
            into.append(
                pltpu.make_async_copy(
                    history_ref.at[user, :, here], parts.at[index, kind], sems.at[index, kind]
                )
            )
    last = pltpu.make_async_copy(weight_ref, held_ref, own_sems.at[2])
    for copy in first + into + [last]:
        copy.start()
    for copy in first:
        copy.wait()
    cand = keep_ref[...]
    for group in range(copy_ref.shape[0]):
        copy_ref[group] = cand
    order, back = orders_of(users[...], cand.shape[0])
    order_ref[...] = order
    back_ref[...] = back
    out = []
    for index, out_ref in enumerate(out_refs):
        for kind in range(2):
            into[2 * index + kind].wait()
            out.append(
                pltpu.make_async_copy(
                    parts.at[index, kind], out_ref.at[kind], sems.at[index, kind]
                )
            )
            out[-1].start()
    last.wait()
    for copy in out:
        copy.wait()


def after_kernel(*refs):
    pass


def prepare_kernel(owners, first_source, place_ref, length_ref, *rest):
    history_refs, (key_ref, value_ref) = rest[:-2], rest[-2:]
    _, span, width = history_refs[0].shape
    user, _ = role(place_ref[0])
    length = length_ref[user]
    position = lax.broadcasted_iota(jnp.int32, (span, width), 0)
    for index, history_ref in enumerate(history_refs):
        at = slice(index * span, (index + 1) * span)
        live = length - source(place_ref[0], first_source + index, owners) * span
        key_ref[:, at] = history_ref[0].T
        value = history_ref[1]
        for head in range(width // HEAD_DIM):
            keep = (position < live) & head_mask((span, width), head)
            value_ref[head, at, :] = jnp.where(keep, value, jnp.zeros_like(value))


def attend_kernel(rows_now, positions_now, query_ref, keys, masked, *rest):
    *begun_refs, out_ref = rest
    blocks, block_rows, width = query_ref.shape
    heads, positions, _ = masked.shape
    step_blocks = rows_now // block_rows

    def step(index, carry):
        here = pl.ds(index * step_blocks, step_blocks)
        query = query_ref[here].reshape(rows_now, width)
        if begun_refs:
            total = begun_refs[0][here].reshape(rows_now, width)
        else:
            total = jnp.zeros((rows_now, width), jnp.float32)
        for start in range(0, positions, positions_now):
            at = slice(start, start + positions_now)
            for head in range(heads):
                own = jnp.where(
                    head_mask((rows_now, width), head), query, jnp.zeros_like(query)
                )
                half = jnp.dot(own, keys[:, at], preferred_element_type=jnp.float32)
                weight = (half + half * jnp.tanh(half)).astype(jnp.bfloat16)
                total += jnp.dot(
                    weight, masked[head, at, :], preferred_element_type=jnp.float32
                )
        out_ref[here] = total.astype(out_ref.dtype).reshape(step_blocks, block_rows, width)
        return carry

    lax.fori_loop(0, blocks // step_blocks, step, 0)


def finish_kernel(
    length_ref, back_ref, partial_ref, gate_ref, source_ref, out_ref, weight_ref, sem
):
    rows, width = gate_ref.shape
    fetch = pltpu.make_async_copy(source_ref, weight_ref, sem)
    fetch.start()
    sums = {}
    for block in range(partial_ref.shape[0]):
        term = partial_ref[block].astype(jnp.float32)
        sums[role(block)] = sums[role(block)] + term if role(block) in sums else term
    total = jnp.concatenate(
        [jnp.concatenate([sums[user, half] for half in range(2)], axis=1) for user in range(USERS)],
        axis=0,
    )
    row = lax.broadcasted_iota(jnp.int32, (rows, width), 0)
    length = jnp.where(row < rows // USERS, length_ref[0], length_ref[1]).astype(jnp.float32)
    attn = total / length
    square = attn * attn
    mean = jnp.zeros((rows, width), jnp.float32)
    for head in range(width // HEAD_DIM):
        mask = head_mask((rows, width), head)
        summed = jnp.sum(jnp.where(mask, square, 0.0), axis=1, keepdims=True)
        mean = jnp.where(mask, summed * (1.0 / HEAD_DIM), mean)
    normed = attn * lax.rsqrt(mean + 1e-06)
    gated = (normed * gate_ref[...]).astype(jnp.bfloat16)
    gated = jnp.dot(back_ref[...], gated, preferred_element_type=jnp.float32).astype(jnp.bfloat16)
    fetch.wait()
    for part in range(out_ref.shape[0]):
        out_ref[part] = jnp.dot(
            gated,
            weight_ref[:, part * width : (part + 1) * width],
            preferred_element_type=jnp.float32,
        ).astype(out_ref.dtype)


def add_kernel(cand_ref, term_ref, out_ref):
    total = cand_ref[...].astype(jnp.float32)
    for group in range(term_ref.shape[0]):
        total += term_ref[group].astype(jnp.float32)
    out_ref[...] = total.astype(out_ref.dtype)


def in_hbm(array):
    return pltpu.with_memory_space_constraint(array, pltpu.HBM)


def local(cand_rows, qu_weight, out_weight, keys, values, lengths, cand_user):
    rows, depth = cand_rows.shape
    width = qu_weight.shape[2]
    positions = keys.shape[1]
    groups = lax.axis_size("head")
    owners = lax.axis_size("seq")
    place = jnp.reshape(lax.axis_index("seq"), (1,)).astype(jnp.int32)
    block_rows, lanes = rows // USERS, width // 2

    *shares, copies, kept, order, back, weight = pl.pallas_call(
        functools.partial(share_kernel, owners),
        out_shape=[pltpu.HBM((2, positions, lanes), jnp.bfloat16)] * SOURCES
        + [
            jax.ShapeDtypeStruct((groups, rows, depth), jnp.bfloat16),
            pltpu.VMEM((rows, depth), jnp.bfloat16),
            pltpu.VMEM((rows, rows), jnp.bfloat16),
            pltpu.VMEM((rows, rows), jnp.bfloat16),
            pltpu.VMEM(qu_weight.shape, jnp.bfloat16),
        ],
        in_specs=[SMEM] + [HBM] * 5,
        out_specs=[HBM] * SOURCES + [VMEM] * 5,
        scratch_shapes=[
            pltpu.VMEM((1, rows), jnp.int32),
            pltpu.VMEM((SOURCES, 2, positions, lanes), jnp.bfloat16),
            pltpu.SemaphoreType.DMA((SOURCES, 2)),
            pltpu.SemaphoreType.DMA((3,)),
        ],
        compiler_params=PARAMS,
        name="share",
    )(place, *map(in_hbm, (cand_user.reshape(1, rows), cand_rows, qu_weight, keys, values)))
    def from_source(index, share):
        return lax.ppermute(
            share, "seq", [(s, source(s, index, owners)) for s in range(owners)]
        )

    early = [shares[0], from_source(1, shares[1])]
    cand_parts = lax.all_to_all(copies, "head", 0, 0, tiled=True)
    queries, gates = pl.pallas_call(
        project_kernel,
        out_shape=(
            jax.ShapeDtypeStruct((owners, block_rows, lanes), jnp.bfloat16),
            jax.ShapeDtypeStruct((rows, width), jnp.bfloat16),
        ),
        in_specs=[VMEM] * 3,
        out_specs=(VMEM, VMEM),
        compiler_params=PARAMS,
        name="project",
    )(
        order,
        cand_parts,
        weight.reshape(qu_weight.shape[0], 2 * width),
    )
    sent = queries
    queries = lax.all_to_all(sent, "seq", 0, 0, tiled=True)
    held = pl.pallas_call(
        after_kernel,
        out_shape=[pltpu.HBM(share.shape, share.dtype) for share in shares[2:]],
        in_specs=[HBM] * (SOURCES - 1),
        out_specs=[HBM] * (SOURCES - 2),
        input_output_aliases={0: 0, 1: 1},
        compiler_params=PARAMS,
        name="after",
    )(*map(in_hbm, shares[2:]), in_hbm(sent))
    late = [from_source(2 + index, share) for index, share in enumerate(held)]

    def prepare(first_source, history):
        count = len(history) * positions
        return pl.pallas_call(
            functools.partial(prepare_kernel, owners, first_source),
            out_shape=(
                jax.ShapeDtypeStruct((lanes, count), jnp.bfloat16),
                jax.ShapeDtypeStruct((lanes // HEAD_DIM, count, lanes), jnp.bfloat16),
            ),
            in_specs=[SMEM] * 2 + [VMEM] * len(history),
            out_specs=(VMEM, VMEM),
            compiler_params=PARAMS,
            name="prepare",
        )(place, lengths, *map(in_hbm, history))

    def attend(dtype, *operands):
        return pl.pallas_call(
            functools.partial(attend_kernel, 1024, 256),
            out_shape=jax.ShapeDtypeStruct((owners, block_rows, lanes), dtype),
            in_specs=[VMEM] * len(operands),
            out_specs=VMEM,
            compiler_params=ATTEND_PARAMS,
            cost_estimate=pl.CostEstimate(
                flops=8 * owners * block_rows * lanes * 2 * positions,
                bytes_accessed=0,
                transcendentals=0,
            ),
            name="attend",
        )(*operands)

    begun = attend(jnp.float32, queries, *prepare(0, early))
    totals = attend(jnp.bfloat16, queries, *prepare(2, late), begun)
    totals = lax.all_to_all(totals, "seq", 0, 0, tiled=True)
    terms = pl.pallas_call(
        finish_kernel,
        out_shape=jax.ShapeDtypeStruct((groups, rows, depth), jnp.bfloat16),
        in_specs=[SMEM] + [VMEM] * 3 + [HBM],
        out_specs=VMEM,
        scratch_shapes=[pltpu.VMEM(out_weight.shape, jnp.bfloat16), pltpu.SemaphoreType.DMA],
        compiler_params=PARAMS,
        name="finish",
    )(lengths, back, totals, gates.astype(jnp.float32), in_hbm(out_weight))
    terms = lax.all_to_all(terms, "head", 0, 0, tiled=True)
    return pl.pallas_call(
        add_kernel,
        out_shape=jax.ShapeDtypeStruct((rows, depth), cand_rows.dtype),
        in_specs=[VMEM, VMEM],
        out_specs=VMEM,
        compiler_params=PARAMS,
        name="add",
    )(kept, terms)


def solution(mesh):
    return jax.shard_map(
        local,
        mesh=mesh,
        in_specs=(
            P(("user", "seq"), "head"),
            P(None, None, "head"),
            P("head", None),
            P("user", "seq", "head"),
            P("user", "seq", "head"),
            P("user"),
            P(("user", "seq")),
        ),
        out_specs=P(("user", "seq"), "head"),
        check_vma=False,
    )
```

```python
import functools

import jax
import jax.numpy as jnp
from jax import lax
from jax.experimental import pallas as pl
from jax.experimental.pallas import tpu as pltpu
from jax.sharding import PartitionSpec as P

HEAD_DIM = 64
USERS = 2
VMEM = pl.BlockSpec(memory_space=pltpu.VMEM)
SMEM = pl.BlockSpec(memory_space=pltpu.SMEM)
HBM = pl.BlockSpec(memory_space=pltpu.HBM)
PARAMS = pltpu.CompilerParams(vmem_limit_bytes=16 * 2**20)
ATTEND_PARAMS = pltpu.CompilerParams(vmem_limit_bytes=24 * 2**20)


SOURCES = 4


def role(place):
    return (place // 4) % 2, (place // 8 + place) % 2


def source(place, index, owners):
    if index == 0:
        return place
    if index == 3:
        return place + 1 - 2 * (place % 2)
    step = 4 - 8 * ((place // 4) % 2)
    return (place + (step if index == 1 else -step) + owners) % owners


def head_mask(shape, head):
    lane = lax.broadcasted_iota(jnp.int32, shape, len(shape) - 1)
    return (lane >= head * HEAD_DIM) & (lane < (head + 1) * HEAD_DIM)


def orders_of(users, rows):
    first = lax.broadcasted_iota(jnp.int32, (rows, rows), 0)
    second = lax.broadcasted_iota(jnp.int32, (rows, rows), 1)
    users = jnp.broadcast_to(users, (rows, rows))
    before = jnp.dot(
        users.astype(jnp.bfloat16),
        (first < second).astype(jnp.bfloat16),
        preferred_element_type=jnp.float32,
    ).astype(jnp.int32)
    target = jnp.where(users > 0, rows // USERS + before, second - before)
    order = (target == first).astype(jnp.float32)
    return order.astype(jnp.bfloat16), order.T.astype(jnp.bfloat16)


def project_kernel(cand_ref, weight_ref, query_ref, gate_ref):
    slices, rows, depth = cand_ref.shape
    width = weight_ref.shape[1] // 2
    total = jnp.zeros((rows, 2 * width), jnp.float32)
    for part in range(slices):
        total += jnp.dot(
            cand_ref[part],
            weight_ref[part * depth : (part + 1) * depth, :],
            preferred_element_type=jnp.float32,
        )
    projected = (total / (1.0 + jnp.exp(-total))).astype(jnp.bfloat16)
    query = (projected[:, :width].astype(jnp.float32) * (0.5 * HEAD_DIM**-0.5)).astype(
        jnp.bfloat16
    )
    _, block_rows, lanes = query_ref.shape
    for owner in range(query_ref.shape[0]):
        user, half = role(owner)
        query_ref[owner] = query[
            user * block_rows : (user + 1) * block_rows, half * lanes : (half + 1) * lanes
        ]
    gate_ref[...] = projected[:, width:]


def part_of(history_ref, user, half, lanes):
    return history_ref.at[user, :, pl.ds(pl.multiple_of(half * lanes, lanes), lanes)]


def share_kernel(
    owners, place_ref, user_ref, cand_ref, weight_ref, key_ref, value_ref, *rest
):
    out_refs, rest = rest[: SOURCES - 1], rest[SOURCES - 1 :]
    copy_ref, keep_ref, held_ref, users, rows, parts, sems, copy_sems, own_sems = rest
    lanes = out_refs[0].shape[2]
    first = [
        pltpu.make_async_copy(cand_ref, keep_ref, own_sems.at[0]),
        pltpu.make_async_copy(user_ref, users, own_sems.at[1]),
    ]
    into = []
    for index in range(SOURCES - 1):
        user, half = role(source(place_ref[0], index + 1, owners))
        for kind, history_ref in enumerate((key_ref, value_ref)):
            into.append(
                pltpu.make_async_copy(
                    part_of(history_ref, user, half, lanes),
                    parts.at[index, kind],
                    sems.at[index, kind],
                )
            )
    last = pltpu.make_async_copy(weight_ref, held_ref, own_sems.at[2])
    for copy in first + into + [last]:
        copy.start()
    for copy in first:
        copy.wait()
    order, _ = orders_of(users[...], rows.shape[0])
    rows[...] = jnp.dot(order, keep_ref[...], preferred_element_type=jnp.float32).astype(
        rows.dtype
    )
    out = []
    for group in range(copy_ref.shape[0]):
        out.append(pltpu.make_async_copy(rows, copy_ref.at[group], copy_sems.at[group]))
        out[-1].start()
    for index, out_ref in enumerate(out_refs):
        for kind in range(2):
            into[2 * index + kind].wait()
            out.append(
                pltpu.make_async_copy(
                    parts.at[index, kind], out_ref.at[kind], sems.at[index, kind]
                )
            )
            out[-1].start()
    last.wait()
    for copy in out:
        copy.wait()


def prepare_kernel(
    owners, place_ref, length_ref, user_ref, key_ref, value_ref, *rest
):
    history_refs, rest = rest[: SOURCES - 1], rest[SOURCES - 1 :]
    turned_ref, masked_ref, back_ref, own, sems = rest
    _, span, width = own.shape
    user, half = role(place_ref[0])
    copies = [
        pltpu.make_async_copy(part_of(history_ref, user, half, width), own.at[kind], sems.at[kind])
        for kind, history_ref in enumerate((key_ref, value_ref))
    ]
    for copy in copies:
        copy.start()
    _, back = orders_of(user_ref[...], back_ref.shape[0])
    back_ref[...] = back
    length = length_ref[user]
    position = lax.broadcasted_iota(jnp.int32, (span, width), 0)
    for index in reversed(range(SOURCES)):
        if index == 0:
            for copy in copies:
                copy.wait()
        history_ref = history_refs[index - 1] if index else own
        at = slice(index * span, (index + 1) * span)
        live = length - source(place_ref[0], index, owners) * span
        turned_ref[:, at] = history_ref[0].T
        value = history_ref[1]
        for head in range(width // HEAD_DIM):
            keep = (position < live) & head_mask((span, width), head)
            masked_ref[head, at, :] = jnp.where(keep, value, jnp.zeros_like(value))


def attend_kernel(rows_now, positions_now, query_ref, keys, masked, out_ref):
    blocks, block_rows, width = query_ref.shape
    heads, positions, _ = masked.shape
    step_blocks = rows_now // block_rows

    def step(index, carry):
        here = pl.ds(index * step_blocks, step_blocks)
        query = query_ref[here].reshape(rows_now, width)
        total = jnp.zeros((rows_now, width), jnp.float32)
        for start in range(0, positions, positions_now):
            at = slice(start, start + positions_now)
            for head in range(heads):
                own = jnp.where(
                    head_mask((rows_now, width), head), query, jnp.zeros_like(query)
                )
                half = jnp.dot(own, keys[:, at], preferred_element_type=jnp.float32)
                weight = (half + half * jnp.tanh(half)).astype(jnp.bfloat16)
                total += jnp.dot(
                    weight, masked[head, at, :], preferred_element_type=jnp.float32
                )
        out_ref[here] = total.astype(jnp.bfloat16).reshape(step_blocks, block_rows, width)
        return carry

    lax.fori_loop(0, blocks // step_blocks, step, 0)


def finish_kernel(length_ref, back_ref, partial_ref, gate_ref, weight_ref, out_ref):
    rows, width = gate_ref.shape
    sums = {}
    for block in range(partial_ref.shape[0]):
        term = partial_ref[block].astype(jnp.float32)
        sums[role(block)] = sums[role(block)] + term if role(block) in sums else term
    total = jnp.concatenate(
        [jnp.concatenate([sums[user, half] for half in range(2)], axis=1) for user in range(USERS)],
        axis=0,
    )
    row = lax.broadcasted_iota(jnp.int32, (rows, width), 0)
    length = jnp.where(row < rows // USERS, length_ref[0], length_ref[1]).astype(jnp.float32)
    attn = total / length
    square = attn * attn
    mean = jnp.zeros((rows, width), jnp.float32)
    for head in range(width // HEAD_DIM):
        mask = head_mask((rows, width), head)
        summed = jnp.sum(jnp.where(mask, square, 0.0), axis=1, keepdims=True)
        mean = jnp.where(mask, summed * (1.0 / HEAD_DIM), mean)
    normed = attn * lax.rsqrt(mean + 1e-06)
    gated = (normed * gate_ref[...]).astype(jnp.bfloat16)
    gated = jnp.dot(back_ref[...], gated, preferred_element_type=jnp.float32).astype(jnp.bfloat16)
    for part in range(out_ref.shape[0]):
        out_ref[part] = jnp.dot(
            gated,
            weight_ref[part],
            preferred_element_type=jnp.float32,
        ).astype(out_ref.dtype)


def add_kernel(cand_ref, term_ref, out_ref):
    total = cand_ref[...].astype(jnp.float32)
    for group in range(term_ref.shape[0]):
        total += term_ref[group].astype(jnp.float32)
    out_ref[...] = total.astype(out_ref.dtype)


def in_hbm(array):
    return pltpu.with_memory_space_constraint(array, pltpu.HBM)


def local(cand_rows, qu_weight, out_weight, keys, values, lengths, cand_user):
    rows, depth = cand_rows.shape
    width = qu_weight.shape[2]
    positions = keys.shape[1]
    groups = lax.axis_size("head")
    owners = lax.axis_size("seq")
    place = jnp.reshape(lax.axis_index("seq"), (1,)).astype(jnp.int32)
    block_rows, lanes = rows // USERS, width // 2

    users = cand_user.reshape(1, rows)
    *shares, copies, kept, weight = pl.pallas_call(
        functools.partial(share_kernel, owners),
        out_shape=[pltpu.HBM((2, positions, lanes), jnp.bfloat16)] * (SOURCES - 1)
        + [
            pltpu.HBM((groups, rows, depth), jnp.bfloat16),
            pltpu.VMEM((rows, depth), jnp.bfloat16),
            pltpu.VMEM(qu_weight.shape, jnp.bfloat16),
        ],
        in_specs=[SMEM] + [HBM] * 5,
        out_specs=[HBM] * SOURCES + [VMEM] * 2,
        scratch_shapes=[
            pltpu.VMEM((1, rows), jnp.int32),
            pltpu.VMEM((rows, depth), jnp.bfloat16),
            pltpu.VMEM((SOURCES - 1, 2, positions, lanes), jnp.bfloat16),
            pltpu.SemaphoreType.DMA((SOURCES - 1, 2)),
            pltpu.SemaphoreType.DMA((groups,)),
            pltpu.SemaphoreType.DMA((3,)),
        ],
        compiler_params=PARAMS,
        name="share",
    )(place, *map(in_hbm, (users, cand_rows, qu_weight, keys, values)))
    history = [
        lax.ppermute(share, "seq", [(s, source(s, index + 1, owners)) for s in range(owners)])
        for index, share in enumerate(shares)
    ]

    cand_parts = lax.all_to_all(copies, "head", 0, 0, tiled=True)
    queries, gates = pl.pallas_call(
        project_kernel,
        out_shape=(
            jax.ShapeDtypeStruct((owners, block_rows, lanes), jnp.bfloat16),
            jax.ShapeDtypeStruct((rows, width), jnp.bfloat16),
        ),
        in_specs=[VMEM] * 2,
        out_specs=(VMEM, VMEM),
        compiler_params=PARAMS,
        name="project",
    )(
        cand_parts,
        weight.reshape(qu_weight.shape[0], 2 * width),
    )
    queries = lax.all_to_all(queries, "seq", 0, 0, tiled=True)
    turned, masked, back = pl.pallas_call(
        functools.partial(prepare_kernel, owners),
        out_shape=(
            jax.ShapeDtypeStruct((lanes, SOURCES * positions), jnp.bfloat16),
            jax.ShapeDtypeStruct(
                (lanes // HEAD_DIM, SOURCES * positions, lanes), jnp.bfloat16
            ),
            pltpu.VMEM((rows, rows), jnp.bfloat16),
        ),
        in_specs=[SMEM] * 2 + [VMEM] + [HBM] * 2 + [VMEM] * (SOURCES - 1),
        out_specs=(VMEM,) * 3,
        scratch_shapes=[
            pltpu.VMEM((2, positions, lanes), jnp.bfloat16),
            pltpu.SemaphoreType.DMA((2,)),
        ],
        compiler_params=PARAMS,
        name="prepare",
    )(place, lengths, *map(in_hbm, (users, keys, values, *history)))
    totals = pl.pallas_call(
        functools.partial(attend_kernel, 1024, 256),
        out_shape=jax.ShapeDtypeStruct((owners, block_rows, lanes), jnp.bfloat16),
        in_specs=[VMEM] * 3,
        out_specs=VMEM,
        compiler_params=ATTEND_PARAMS,
        name="attend",
    )(queries, turned, masked)
    totals = lax.all_to_all(totals, "seq", 0, 0, tiled=True)
    blocks = jnp.transpose(out_weight.reshape(width, groups, depth), (1, 0, 2))
    terms = pl.pallas_call(
        finish_kernel,
        out_shape=jax.ShapeDtypeStruct((groups, rows, depth), jnp.bfloat16),
        in_specs=[SMEM] + [VMEM] * 4,
        out_specs=VMEM,
        compiler_params=PARAMS,
        name="finish",
    )(lengths, back, totals, gates.astype(jnp.float32), blocks)
    terms = lax.all_to_all(terms, "head", 0, 0, tiled=True)
    return pl.pallas_call(
        add_kernel,
        out_shape=jax.ShapeDtypeStruct((rows, depth), cand_rows.dtype),
        in_specs=[VMEM, VMEM],
        out_specs=VMEM,
        compiler_params=PARAMS,
        name="add",
    )(kept, terms)


def solution(mesh):
    return jax.shard_map(
        local,
        mesh=mesh,
        in_specs=(
            P(("user", "seq"), "head"),
            P(None, None, "head"),
            P("head", None),
            P("user", "seq", "head"),
            P("user", "seq", "head"),
            P("user"),
            P(("user", "seq")),
        ),
        out_specs=P(("user", "seq"), "head"),
        check_vma=False,
    )
```

```python
import functools

import jax
import jax.numpy as jnp
from jax import lax
from jax.experimental import pallas as pl
from jax.experimental.pallas import tpu as pltpu
from jax.sharding import PartitionSpec as P

HEAD_DIM = 64
USERS = 2
VMEM = pl.BlockSpec(memory_space=pltpu.VMEM)
SMEM = pl.BlockSpec(memory_space=pltpu.SMEM)
HBM = pl.BlockSpec(memory_space=pltpu.HBM)
PARAMS = pltpu.CompilerParams(vmem_limit_bytes=16 * 2**20)
ATTEND_PARAMS = pltpu.CompilerParams(vmem_limit_bytes=24 * 2**20)


SOURCES = 4
ATTEND_TILE = (1024, 256)


def role(place):
    return (place // 4) % 2, (place // 8 + place) % 2


def source(place, index, owners):
    if index == 0:
        return place
    if index == 3:
        return place + 1 - 2 * (place % 2)
    step = 4 - 8 * ((place // 4) % 2)
    return (place + (step if index == 1 else -step) + owners) % owners


def head_mask(shape, head):
    lane = lax.broadcasted_iota(jnp.int32, shape, len(shape) - 1)
    return (lane >= head * HEAD_DIM) & (lane < (head + 1) * HEAD_DIM)


def orders_of(users, rows):
    first = lax.broadcasted_iota(jnp.int32, (rows, rows), 0)
    second = lax.broadcasted_iota(jnp.int32, (rows, rows), 1)
    users = jnp.broadcast_to(users, (rows, rows))
    before = jnp.dot(
        users.astype(jnp.bfloat16),
        (first < second).astype(jnp.bfloat16),
        preferred_element_type=jnp.float32,
    ).astype(jnp.int32)
    target = jnp.where(users > 0, rows // USERS + before, second - before)
    order = (target == first).astype(jnp.float32)
    return order.astype(jnp.bfloat16), order.T.astype(jnp.bfloat16)


def project_kernel(cand_ref, weight_ref, query_ref, gate_ref):
    slices, rows, depth = cand_ref.shape
    width = weight_ref.shape[1] // 2
    total = jnp.zeros((rows, 2 * width), jnp.float32)
    for part in range(slices):
        total += jnp.dot(
            cand_ref[part],
            weight_ref[part * depth : (part + 1) * depth, :],
            preferred_element_type=jnp.float32,
        )
    projected = (total / (1.0 + jnp.exp(-total))).astype(jnp.bfloat16)
    query = (projected[:, :width].astype(jnp.float32) * (0.5 * HEAD_DIM**-0.5)).astype(
        jnp.bfloat16
    )
    _, block_rows, lanes = query_ref.shape
    for owner in range(query_ref.shape[0]):
        user, half = role(owner)
        query_ref[owner] = query[
            user * block_rows : (user + 1) * block_rows, half * lanes : (half + 1) * lanes
        ]
    gate_ref[...] = projected[:, width:]


def part_of(history_ref, user, half, lanes):
    return history_ref.at[user, :, pl.ds(pl.multiple_of(half * lanes, lanes), lanes)]


def share_kernel(
    owners, place_ref, user_ref, cand_ref, weight_ref, key_ref, value_ref, *rest
):
    out_refs, rest = rest[: SOURCES - 1], rest[SOURCES - 1 :]
    copy_ref, keep_ref, held_ref, users, rows, parts, sems, copy_sems, own_sems = rest
    lanes = out_refs[0].shape[2]
    first = [
        pltpu.make_async_copy(cand_ref, keep_ref, own_sems.at[0]),
        pltpu.make_async_copy(user_ref, users, own_sems.at[1]),
    ]
    into = []
    for index in range(SOURCES - 1):
        user, half = role(source(place_ref[0], index + 1, owners))
        for kind, history_ref in enumerate((key_ref, value_ref)):
            into.append(
                pltpu.make_async_copy(
                    part_of(history_ref, user, half, lanes),
                    parts.at[index, kind],
                    sems.at[index, kind],
                )
            )
    last = pltpu.make_async_copy(weight_ref, held_ref, own_sems.at[2])
    for copy in first + into + [last]:
        copy.start()
    for copy in first:
        copy.wait()
    order, _ = orders_of(users[...], rows.shape[0])
    rows[...] = jnp.dot(order, keep_ref[...], preferred_element_type=jnp.float32).astype(
        rows.dtype
    )
    out = []
    for group in range(copy_ref.shape[0]):
        out.append(pltpu.make_async_copy(rows, copy_ref.at[group], copy_sems.at[group]))
        out[-1].start()
    for index, out_ref in enumerate(out_refs):
        for kind in range(2):
            into[2 * index + kind].wait()
            out.append(
                pltpu.make_async_copy(
                    parts.at[index, kind], out_ref.at[kind], sems.at[index, kind]
                )
            )
            out[-1].start()
    last.wait()
    for copy in out:
        copy.wait()


def after_kernel(*refs):
    pass


def prepare_source(index, owners, place, length, history_ref, at, turned_ref, live_ref):
    _, span, width = history_ref.shape
    position = lax.broadcasted_iota(jnp.int32, (span, width), 0)
    live = length - source(place, index, owners) * span
    turned_ref[:, at] = history_ref[0].T
    value = history_ref[1]
    live_ref[at, :] = jnp.where(position < live, value, jnp.zeros_like(value))


def prepare_kernel(
    owners, place_ref, length_ref, user_ref, key_ref, value_ref, *rest
):
    *history_refs, turned_ref, live_ref, back_ref, own, sems = rest
    _, span, width = own.shape
    user, half = role(place_ref[0])
    copies = [
        pltpu.make_async_copy(part_of(history_ref, user, half, width), own.at[kind], sems.at[kind])
        for kind, history_ref in enumerate((key_ref, value_ref))
    ]
    for copy in copies:
        copy.start()
    _, back = orders_of(user_ref[...], back_ref.shape[0])
    back_ref[...] = back
    for index in reversed(range(SOURCES - 1)):
        if index == 0:
            for copy in copies:
                copy.wait()
        prepare_source(
            index,
            owners,
            place_ref[0],
            length_ref[user],
            history_refs[index - 1] if index else own,
            slice(index * span, (index + 1) * span),
            turned_ref,
            live_ref,
        )


def attend_rows(rows_now, positions_now, query_ref, keys, values, begun_ref, out_ref):
    blocks, block_rows, width = query_ref.shape
    positions = values.shape[0]
    step_blocks = rows_now // block_rows

    def of_head(array, head):
        return jnp.where(head_mask(array.shape, head), array, jnp.zeros_like(array))

    def step(index, carry):
        here = pl.ds(index * step_blocks, step_blocks)
        query = query_ref[here].reshape(rows_now, width)
        if begun_ref is None:
            total = jnp.zeros((rows_now, width), jnp.float32)
        else:
            total = begun_ref[here].reshape(rows_now, width)
        for start in range(0, positions, positions_now):
            at = slice(start, start + positions_now)
            for head in range(width // HEAD_DIM):
                half = jnp.dot(
                    of_head(query, head), keys[:, at], preferred_element_type=jnp.float32
                )
                weight = (half + half * jnp.tanh(half)).astype(jnp.bfloat16)
                total += jnp.dot(
                    weight, of_head(values[at, :], head), preferred_element_type=jnp.float32
                )
        out_ref[here] = total.astype(out_ref.dtype).reshape(step_blocks, block_rows, width)
        return carry

    lax.fori_loop(0, blocks // step_blocks, step, 0)


def begin_kernel(query_ref, keys, values, out_ref):
    attend_rows(*ATTEND_TILE, query_ref, keys, values, None, out_ref)


def end_kernel(
    owners, place_ref, length_ref, query_ref, history_ref, begun_ref, out_ref, keys, values
):
    user, _ = role(place_ref[0])
    span = history_ref.shape[1]
    prepare_source(
        SOURCES - 1,
        owners,
        place_ref[0],
        length_ref[user],
        history_ref,
        slice(0, span),
        keys,
        values,
    )
    attend_rows(*ATTEND_TILE, query_ref, keys, values, begun_ref, out_ref)


def finish_kernel(length_ref, back_ref, partial_ref, gate_ref, weight_ref, out_ref):
    rows, width = gate_ref.shape
    sums = {}
    for block in range(partial_ref.shape[0]):
        term = partial_ref[block].astype(jnp.float32)
        sums[role(block)] = sums[role(block)] + term if role(block) in sums else term
    total = jnp.concatenate(
        [jnp.concatenate([sums[user, half] for half in range(2)], axis=1) for user in range(USERS)],
        axis=0,
    )
    row = lax.broadcasted_iota(jnp.int32, (rows, width), 0)
    length = jnp.where(row < rows // USERS, length_ref[0], length_ref[1]).astype(jnp.float32)
    attn = total / length
    square = attn * attn
    mean = jnp.zeros((rows, width), jnp.float32)
    for head in range(width // HEAD_DIM):
        mask = head_mask((rows, width), head)
        summed = jnp.sum(jnp.where(mask, square, 0.0), axis=1, keepdims=True)
        mean = jnp.where(mask, summed * (1.0 / HEAD_DIM), mean)
    normed = attn * lax.rsqrt(mean + 1e-06)
    gated = (normed * gate_ref[...]).astype(jnp.bfloat16)
    gated = jnp.dot(back_ref[...], gated, preferred_element_type=jnp.float32).astype(jnp.bfloat16)
    for part in range(out_ref.shape[0]):
        out_ref[part] = jnp.dot(
            gated,
            weight_ref[part],
            preferred_element_type=jnp.float32,
        ).astype(out_ref.dtype)


def add_kernel(cand_ref, term_ref, out_ref):
    total = cand_ref[...].astype(jnp.float32)
    for group in range(term_ref.shape[0]):
        total += term_ref[group].astype(jnp.float32)
    out_ref[...] = total.astype(out_ref.dtype)


def in_hbm(array):
    return pltpu.with_memory_space_constraint(array, pltpu.HBM)


def local(cand_rows, qu_weight, out_weight, keys, values, lengths, cand_user):
    rows, depth = cand_rows.shape
    width = qu_weight.shape[2]
    positions = keys.shape[1]
    groups = lax.axis_size("head")
    owners = lax.axis_size("seq")
    place = jnp.reshape(lax.axis_index("seq"), (1,)).astype(jnp.int32)
    block_rows, lanes = rows // USERS, width // 2

    users = cand_user.reshape(1, rows)
    *shares, copies, kept, weight = pl.pallas_call(
        functools.partial(share_kernel, owners),
        out_shape=[pltpu.HBM((2, positions, lanes), jnp.bfloat16)] * (SOURCES - 1)
        + [
            pltpu.HBM((groups, rows, depth), jnp.bfloat16),
            pltpu.VMEM((rows, depth), jnp.bfloat16),
            pltpu.VMEM(qu_weight.shape, jnp.bfloat16),
        ],
        in_specs=[SMEM] + [HBM] * 5,
        out_specs=[HBM] * SOURCES + [VMEM] * 2,
        scratch_shapes=[
            pltpu.VMEM((1, rows), jnp.int32),
            pltpu.VMEM((rows, depth), jnp.bfloat16),
            pltpu.VMEM((SOURCES - 1, 2, positions, lanes), jnp.bfloat16),
            pltpu.SemaphoreType.DMA((SOURCES - 1, 2)),
            pltpu.SemaphoreType.DMA((groups,)),
            pltpu.SemaphoreType.DMA((3,)),
        ],
        compiler_params=PARAMS,
        name="share",
    )(place, *map(in_hbm, (users, cand_rows, qu_weight, keys, values)))
    def from_source(index, share):
        return lax.ppermute(
            share, "seq", [(s, source(s, index, owners)) for s in range(owners)]
        )

    along_z = [from_source(index + 1, share) for index, share in enumerate(shares[:-1])]

    cand_parts = lax.all_to_all(copies, "head", 0, 0, tiled=True)
    queries, gates = pl.pallas_call(
        project_kernel,
        out_shape=(
            pltpu.HBM((owners, block_rows, lanes), jnp.bfloat16),
            jax.ShapeDtypeStruct((rows, width), jnp.bfloat16),
        ),
        in_specs=[VMEM] * 2,
        out_specs=(VMEM, VMEM),
        compiler_params=PARAMS,
        name="project",
    )(
        cand_parts,
        weight.reshape(qu_weight.shape[0], 2 * width),
    )
    share = pl.pallas_call(
        after_kernel,
        out_shape=pltpu.HBM(shares[-1].shape, shares[-1].dtype),
        in_specs=[HBM] * 2,
        out_specs=HBM,
        input_output_aliases={0: 0},
        compiler_params=PARAMS,
        name="after",
    )(in_hbm(shares[-1]), in_hbm(queries))
    along_y = from_source(SOURCES - 1, share)
    queries = lax.all_to_all(queries, "seq", 0, 0, tiled=True)
    count = (SOURCES - 1) * positions
    turned, live, back = pl.pallas_call(
        functools.partial(prepare_kernel, owners),
        out_shape=(
            jax.ShapeDtypeStruct((lanes, count), jnp.bfloat16),
            jax.ShapeDtypeStruct((count, lanes), jnp.bfloat16),
            pltpu.VMEM((rows, rows), jnp.bfloat16),
        ),
        in_specs=[SMEM] * 2 + [VMEM] + [HBM] * 2 + [VMEM] * (SOURCES - 2),
        out_specs=(VMEM,) * 3,
        scratch_shapes=[
            pltpu.VMEM((2, positions, lanes), jnp.bfloat16),
            pltpu.SemaphoreType.DMA((2,)),
        ],
        compiler_params=PARAMS,
        name="prepare",
    )(place, lengths, *map(in_hbm, (users, keys, values, *along_z)))
    begun = pl.pallas_call(
        begin_kernel,
        out_shape=jax.ShapeDtypeStruct((owners, block_rows, lanes), jnp.float32),
        in_specs=[VMEM] * 3,
        out_specs=VMEM,
        compiler_params=ATTEND_PARAMS,
        cost_estimate=pl.CostEstimate(
            flops=8 * owners * block_rows * lanes * count, bytes_accessed=0, transcendentals=0
        ),
        name="begin",
    )(queries, turned, live)
    totals = pl.pallas_call(
        functools.partial(end_kernel, owners),
        out_shape=jax.ShapeDtypeStruct((owners, block_rows, lanes), jnp.bfloat16),
        in_specs=[SMEM] * 2 + [VMEM] * 3,
        out_specs=VMEM,
        scratch_shapes=[
            pltpu.VMEM((lanes, positions), jnp.bfloat16),
            pltpu.VMEM((positions, lanes), jnp.bfloat16),
        ],
        compiler_params=ATTEND_PARAMS,
        cost_estimate=pl.CostEstimate(
            flops=8 * owners * block_rows * lanes * positions, bytes_accessed=0, transcendentals=0
        ),
        name="end",
    )(place, lengths, queries, along_y, begun)
    totals = lax.all_to_all(totals, "seq", 0, 0, tiled=True)
    blocks = jnp.transpose(out_weight.reshape(width, groups, depth), (1, 0, 2))
    terms = pl.pallas_call(
        finish_kernel,
        out_shape=jax.ShapeDtypeStruct((groups, rows, depth), jnp.bfloat16),
        in_specs=[SMEM] + [VMEM] * 4,
        out_specs=VMEM,
        compiler_params=PARAMS,
        name="finish",
    )(lengths, back, totals, gates.astype(jnp.float32), blocks)
    terms = lax.all_to_all(terms, "head", 0, 0, tiled=True)
    return pl.pallas_call(
        add_kernel,
        out_shape=jax.ShapeDtypeStruct((rows, depth), cand_rows.dtype),
        in_specs=[VMEM, VMEM],
        out_specs=VMEM,
        compiler_params=PARAMS,
        name="add",
    )(kept, terms)


def solution(mesh):
    return jax.shard_map(
        local,
        mesh=mesh,
        in_specs=(
            P(("user", "seq"), "head"),
            P(None, None, "head"),
            P("head", None),
            P("user", "seq", "head"),
            P("user", "seq", "head"),
            P("user"),
            P(("user", "seq")),
        ),
        out_specs=P(("user", "seq"), "head"),
        check_vma=False,
    )
```

```python
import functools

import jax
import jax.numpy as jnp
from jax import lax
from jax.experimental import pallas as pl
from jax.experimental.pallas import tpu as pltpu
from jax.sharding import PartitionSpec as P

HEAD_DIM = 64
USERS = 2
VMEM = pl.BlockSpec(memory_space=pltpu.VMEM)
SMEM = pl.BlockSpec(memory_space=pltpu.SMEM)
HBM = pl.BlockSpec(memory_space=pltpu.HBM)
PARAMS = pltpu.CompilerParams(vmem_limit_bytes=16 * 2**20)
ATTEND_PARAMS = pltpu.CompilerParams(vmem_limit_bytes=24 * 2**20)


SOURCES = 4


def role(place):
    return (place // 4) % 2, (place // 8 + place) % 2


def source(place, index, owners):
    if index == 0:
        return place
    if index == 3:
        return place + 1 - 2 * (place % 2)
    step = 4 - 8 * ((place // 4) % 2)
    return (place + (step if index == 1 else -step) + owners) % owners


def head_mask(shape, head):
    lane = lax.broadcasted_iota(jnp.int32, shape, len(shape) - 1)
    return (lane >= head * HEAD_DIM) & (lane < (head + 1) * HEAD_DIM)


def orders_of(users, rows):
    first = lax.broadcasted_iota(jnp.int32, (rows, rows), 0)
    second = lax.broadcasted_iota(jnp.int32, (rows, rows), 1)
    users = jnp.broadcast_to(users, (rows, rows))
    before = jnp.dot(
        users.astype(jnp.bfloat16),
        (first < second).astype(jnp.bfloat16),
        preferred_element_type=jnp.float32,
    ).astype(jnp.int32)
    target = jnp.where(users > 0, rows // USERS + before, second - before)
    order = (target == first).astype(jnp.float32)
    return order.astype(jnp.bfloat16), order.T.astype(jnp.bfloat16)


def project_kernel(cand_ref, weight_ref, query_ref, gate_ref):
    slices, rows, depth = cand_ref.shape
    width = weight_ref.shape[1] // 2
    total = jnp.zeros((rows, 2 * width), jnp.float32)
    for part in range(slices):
        total += jnp.dot(
            cand_ref[part],
            weight_ref[part * depth : (part + 1) * depth, :],
            preferred_element_type=jnp.float32,
        )
    projected = (total / (1.0 + jnp.exp(-total))).astype(jnp.bfloat16)
    query = (projected[:, :width].astype(jnp.float32) * (0.5 * HEAD_DIM**-0.5)).astype(
        jnp.bfloat16
    )
    _, block_rows, lanes = query_ref.shape
    for owner in range(query_ref.shape[0]):
        user, half = role(owner)
        query_ref[owner] = query[
            user * block_rows : (user + 1) * block_rows, half * lanes : (half + 1) * lanes
        ]
    gate_ref[...] = projected[:, width:]


def part_of(history_ref, user, half, lanes):
    return history_ref.at[user, :, pl.ds(pl.multiple_of(half * lanes, lanes), lanes)]


def share_kernel(
    owners, place_ref, user_ref, cand_ref, weight_ref, key_ref, value_ref, *rest
):
    out_refs, rest = rest[: SOURCES - 1], rest[SOURCES - 1 :]
    copy_ref, keep_ref, held_ref, users, rows, parts, sems, copy_sems, own_sems = rest
    lanes = out_refs[0].shape[2]
    first = [
        pltpu.make_async_copy(cand_ref, keep_ref, own_sems.at[0]),
        pltpu.make_async_copy(user_ref, users, own_sems.at[1]),
    ]
    into = []
    for index in range(SOURCES - 1):
        user, half = role(source(place_ref[0], index + 1, owners))
        for kind, history_ref in enumerate((key_ref, value_ref)):
            into.append(
                pltpu.make_async_copy(
                    part_of(history_ref, user, half, lanes),
                    parts.at[index, kind],
                    sems.at[index, kind],
                )
            )
    last = pltpu.make_async_copy(weight_ref, held_ref, own_sems.at[2])
    for copy in first + into + [last]:
        copy.start()
    for copy in first:
        copy.wait()
    order, _ = orders_of(users[...], rows.shape[0])
    rows[...] = jnp.dot(order, keep_ref[...], preferred_element_type=jnp.float32).astype(
        rows.dtype
    )
    out = []
    for group in range(copy_ref.shape[0]):
        out.append(pltpu.make_async_copy(rows, copy_ref.at[group], copy_sems.at[group]))
        out[-1].start()
    for index, out_ref in enumerate(out_refs):
        for kind in range(2):
            into[2 * index + kind].wait()
            out.append(
                pltpu.make_async_copy(
                    parts.at[index, kind], out_ref.at[kind], sems.at[index, kind]
                )
            )
            out[-1].start()
    last.wait()
    for copy in out:
        copy.wait()


def prepare_kernel(
    owners, place_ref, length_ref, user_ref, key_ref, value_ref, *rest
):
    history_refs, rest = rest[: SOURCES - 1], rest[SOURCES - 1 :]
    turned_ref, live_ref, back_ref, own, sems = rest
    _, span, width = own.shape
    user, half = role(place_ref[0])
    copies = [
        pltpu.make_async_copy(part_of(history_ref, user, half, width), own.at[kind], sems.at[kind])
        for kind, history_ref in enumerate((key_ref, value_ref))
    ]
    for copy in copies:
        copy.start()
    _, back = orders_of(user_ref[...], back_ref.shape[0])
    back_ref[...] = back
    length = length_ref[user]
    position = lax.broadcasted_iota(jnp.int32, (span, width), 0)
    for index in reversed(range(SOURCES)):
        if index == 0:
            for copy in copies:
                copy.wait()
        history_ref = history_refs[index - 1] if index else own
        at = slice(index * span, (index + 1) * span)
        live = length - source(place_ref[0], index, owners) * span
        turned_ref[:, at] = history_ref[0].T
        value = history_ref[1]
        live_ref[at, :] = jnp.where(position < live, value, jnp.zeros_like(value))


def attend_kernel(rows_now, positions_now, query_ref, keys, values, out_ref):
    blocks, block_rows, width = query_ref.shape
    positions = values.shape[0]
    step_blocks = rows_now // block_rows

    def of_head(array, head):
        return jnp.where(head_mask(array.shape, head), array, jnp.zeros_like(array))

    def step(index, carry):
        here = pl.ds(index * step_blocks, step_blocks)
        query = query_ref[here].reshape(rows_now, width)
        total = jnp.zeros((rows_now, width), jnp.float32)
        for start in range(0, positions, positions_now):
            at = slice(start, start + positions_now)
            for head in range(width // HEAD_DIM):
                half = jnp.dot(
                    of_head(query, head), keys[:, at], preferred_element_type=jnp.float32
                )
                weight = (half + half * jnp.tanh(half)).astype(jnp.bfloat16)
                total += jnp.dot(
                    weight, of_head(values[at, :], head), preferred_element_type=jnp.float32
                )
        out_ref[here] = total.astype(jnp.bfloat16).reshape(step_blocks, block_rows, width)
        return carry

    lax.fori_loop(0, blocks // step_blocks, step, 0)


def finish_kernel(length_ref, back_ref, partial_ref, gate_ref, weight_ref, out_ref):
    rows, width = gate_ref.shape
    sums = {}
    for block in range(partial_ref.shape[0]):
        term = partial_ref[block].astype(jnp.float32)
        sums[role(block)] = sums[role(block)] + term if role(block) in sums else term
    total = jnp.concatenate(
        [jnp.concatenate([sums[user, half] for half in range(2)], axis=1) for user in range(USERS)],
        axis=0,
    )
    row = lax.broadcasted_iota(jnp.int32, (rows, width), 0)
    length = jnp.where(row < rows // USERS, length_ref[0], length_ref[1]).astype(jnp.float32)
    attn = total / length
    square = attn * attn
    mean = jnp.zeros((rows, width), jnp.float32)
    for head in range(width // HEAD_DIM):
        mask = head_mask((rows, width), head)
        summed = jnp.sum(jnp.where(mask, square, 0.0), axis=1, keepdims=True)
        mean = jnp.where(mask, summed * (1.0 / HEAD_DIM), mean)
    normed = attn * lax.rsqrt(mean + 1e-06)
    gated = (normed * gate_ref[...].astype(jnp.float32)).astype(jnp.bfloat16)
    gated = jnp.dot(back_ref[...], gated, preferred_element_type=jnp.float32).astype(jnp.bfloat16)
    for part in range(out_ref.shape[0]):
        out_ref[part] = jnp.dot(
            gated,
            weight_ref[:, part * width : (part + 1) * width],
            preferred_element_type=jnp.float32,
        ).astype(out_ref.dtype)


def add_kernel(cand_ref, term_ref, out_ref):
    total = cand_ref[...].astype(jnp.float32)
    for group in range(term_ref.shape[0]):
        total += term_ref[group].astype(jnp.float32)
    out_ref[...] = total.astype(out_ref.dtype)


def in_hbm(array):
    return pltpu.with_memory_space_constraint(array, pltpu.HBM)


def local(cand_rows, qu_weight, out_weight, keys, values, lengths, cand_user):
    rows, depth = cand_rows.shape
    width = qu_weight.shape[2]
    positions = keys.shape[1]
    groups = lax.axis_size("head")
    owners = lax.axis_size("seq")
    place = jnp.reshape(lax.axis_index("seq"), (1,)).astype(jnp.int32)
    block_rows, lanes = rows // USERS, width // 2

    users = cand_user.reshape(1, rows)
    *shares, copies, kept, weight = pl.pallas_call(
        functools.partial(share_kernel, owners),
        out_shape=[pltpu.HBM((2, positions, lanes), jnp.bfloat16)] * (SOURCES - 1)
        + [
            pltpu.HBM((groups, rows, depth), jnp.bfloat16),
            pltpu.VMEM((rows, depth), jnp.bfloat16),
            pltpu.VMEM(qu_weight.shape, jnp.bfloat16),
        ],
        in_specs=[SMEM] + [HBM] * 5,
        out_specs=[HBM] * SOURCES + [VMEM] * 2,
        scratch_shapes=[
            pltpu.VMEM((1, rows), jnp.int32),
            pltpu.VMEM((rows, depth), jnp.bfloat16),
            pltpu.VMEM((SOURCES - 1, 2, positions, lanes), jnp.bfloat16),
            pltpu.SemaphoreType.DMA((SOURCES - 1, 2)),
            pltpu.SemaphoreType.DMA((groups,)),
            pltpu.SemaphoreType.DMA((3,)),
        ],
        compiler_params=PARAMS,
        name="share",
    )(place, *map(in_hbm, (users, cand_rows, qu_weight, keys, values)))
    history = [
        lax.ppermute(share, "seq", [(s, source(s, index + 1, owners)) for s in range(owners)])
        for index, share in enumerate(shares)
    ]

    cand_parts = lax.all_to_all(copies, "head", 0, 0, tiled=True)
    queries, gates = pl.pallas_call(
        project_kernel,
        out_shape=(
            jax.ShapeDtypeStruct((owners, block_rows, lanes), jnp.bfloat16),
            jax.ShapeDtypeStruct((rows, width), jnp.bfloat16),
        ),
        in_specs=[VMEM] * 2,
        out_specs=(VMEM, VMEM),
        compiler_params=PARAMS,
        name="project",
    )(
        cand_parts,
        weight.reshape(qu_weight.shape[0], 2 * width),
    )
    queries = lax.all_to_all(queries, "seq", 0, 0, tiled=True)
    turned, live, back = pl.pallas_call(
        functools.partial(prepare_kernel, owners),
        out_shape=(
            jax.ShapeDtypeStruct((lanes, SOURCES * positions), jnp.bfloat16),
            jax.ShapeDtypeStruct((SOURCES * positions, lanes), jnp.bfloat16),
            pltpu.VMEM((rows, rows), jnp.bfloat16),
        ),
        in_specs=[SMEM] * 2 + [VMEM] + [HBM] * 2 + [VMEM] * (SOURCES - 1),
        out_specs=(VMEM,) * 3,
        scratch_shapes=[
            pltpu.VMEM((2, positions, lanes), jnp.bfloat16),
            pltpu.SemaphoreType.DMA((2,)),
        ],
        compiler_params=PARAMS,
        name="prepare",
    )(place, lengths, *map(in_hbm, (users, keys, values, *history)))
    totals = pl.pallas_call(
        functools.partial(attend_kernel, 1024, 256),
        out_shape=jax.ShapeDtypeStruct((owners, block_rows, lanes), jnp.bfloat16),
        in_specs=[VMEM] * 3,
        out_specs=VMEM,
        compiler_params=ATTEND_PARAMS,
        name="attend",
    )(queries, turned, live)
    totals = lax.all_to_all(totals, "seq", 0, 0, tiled=True)
    terms = pl.pallas_call(
        finish_kernel,
        out_shape=jax.ShapeDtypeStruct((groups, rows, depth), jnp.bfloat16),
        in_specs=[SMEM] + [VMEM] * 4,
        out_specs=VMEM,
        compiler_params=PARAMS,
        name="finish",
    )(lengths, back, totals, gates, out_weight)
    terms = lax.all_to_all(terms, "head", 0, 0, tiled=True)
    return pl.pallas_call(
        add_kernel,
        out_shape=jax.ShapeDtypeStruct((rows, depth), cand_rows.dtype),
        in_specs=[VMEM, VMEM],
        out_specs=VMEM,
        compiler_params=PARAMS,
        name="add",
    )(kept, terms)


def solution(mesh):
    return jax.shard_map(
        local,
        mesh=mesh,
        in_specs=(
            P(("user", "seq"), "head"),
            P(None, None, "head"),
            P("head", None),
            P("user", "seq", "head"),
            P("user", "seq", "head"),
            P("user"),
            P(("user", "seq")),
        ),
        out_specs=P(("user", "seq"), "head"),
        check_vma=False,
    )
```

```python
import functools

import jax
import jax.numpy as jnp
from jax import lax
from jax.experimental import pallas as pl
from jax.experimental.pallas import tpu as pltpu
from jax.sharding import PartitionSpec as P

HEAD_DIM = 64
USERS = 2
VMEM = pl.BlockSpec(memory_space=pltpu.VMEM)
SMEM = pl.BlockSpec(memory_space=pltpu.SMEM)
HBM = pl.BlockSpec(memory_space=pltpu.HBM)
PARAMS = pltpu.CompilerParams(vmem_limit_bytes=16 * 2**20)
ATTEND_PARAMS = pltpu.CompilerParams(vmem_limit_bytes=24 * 2**20)


SOURCES = 4


def role(place):
    return (place // 4) % 2, (place // 8 + place) % 2


def source(place, index, owners):
    if index == 0:
        return place
    if index == 2:
        return place + 1 - 2 * (place % 2)
    step = 4 - 8 * ((place // 4) % 2)
    return (place + (step if index == 1 else -step) + owners) % owners


def head_mask(shape, head):
    lane = lax.broadcasted_iota(jnp.int32, shape, len(shape) - 1)
    return (lane >= head * HEAD_DIM) & (lane < (head + 1) * HEAD_DIM)


def orders_of(users, rows):
    first = lax.broadcasted_iota(jnp.int32, (rows, rows), 0)
    second = lax.broadcasted_iota(jnp.int32, (rows, rows), 1)
    users = jnp.broadcast_to(users, (rows, rows))
    before = jnp.dot(
        users.astype(jnp.bfloat16),
        (first < second).astype(jnp.bfloat16),
        preferred_element_type=jnp.float32,
    ).astype(jnp.int32)
    target = jnp.where(users > 0, rows // USERS + before, second - before)
    order = (target == first).astype(jnp.float32)
    return order.astype(jnp.bfloat16), order.T.astype(jnp.bfloat16)


def project_kernel(cand_ref, weight_ref, query_ref, gate_ref):
    slices, rows, depth = cand_ref.shape
    width = weight_ref.shape[1] // 2
    total = jnp.zeros((rows, 2 * width), jnp.float32)
    for part in range(slices):
        total += jnp.dot(
            cand_ref[part],
            weight_ref[part * depth : (part + 1) * depth, :],
            preferred_element_type=jnp.float32,
        )
    projected = (total / (1.0 + jnp.exp(-total))).astype(jnp.bfloat16)
    query = (projected[:, :width].astype(jnp.float32) * (0.5 * HEAD_DIM**-0.5)).astype(
        jnp.bfloat16
    )
    _, block_rows, lanes = query_ref.shape
    for owner in range(query_ref.shape[0]):
        user, half = role(owner)
        query_ref[owner] = query[
            user * block_rows : (user + 1) * block_rows, half * lanes : (half + 1) * lanes
        ]
    gate_ref[...] = projected[:, width:]


def part_of(history_ref, user, half, lanes):
    return history_ref.at[user, :, pl.ds(pl.multiple_of(half * lanes, lanes), lanes)]


def share_kernel(
    owners, place_ref, user_ref, cand_ref, weight_ref, key_ref, value_ref, *rest
):
    out_refs, rest = rest[: SOURCES - 1], rest[SOURCES - 1 :]
    copy_ref, keep_ref, held_ref, users, rows, parts, sems, copy_sems, own_sems = rest
    lanes = out_refs[0].shape[2]
    first = [
        pltpu.make_async_copy(cand_ref, keep_ref, own_sems.at[0]),
        pltpu.make_async_copy(user_ref, users, own_sems.at[1]),
    ]
    into = []
    for index in range(SOURCES - 1):
        user, half = role(source(place_ref[0], index + 1, owners))
        for kind, history_ref in enumerate((key_ref, value_ref)):
            into.append(
                pltpu.make_async_copy(
                    part_of(history_ref, user, half, lanes),
                    parts.at[index, kind],
                    sems.at[index, kind],
                )
            )
    last = pltpu.make_async_copy(weight_ref, held_ref, own_sems.at[2])
    for copy in first + into + [last]:
        copy.start()
    for copy in first:
        copy.wait()
    order, _ = orders_of(users[...], rows.shape[0])
    rows[...] = jnp.dot(order, keep_ref[...], preferred_element_type=jnp.float32).astype(
        rows.dtype
    )
    out = []
    for group in range(copy_ref.shape[0]):
        out.append(pltpu.make_async_copy(rows, copy_ref.at[group], copy_sems.at[group]))
        out[-1].start()
    for index, out_ref in enumerate(out_refs):
        for kind in range(2):
            into[2 * index + kind].wait()
            out.append(
                pltpu.make_async_copy(
                    parts.at[index, kind], out_ref.at[kind], sems.at[index, kind]
                )
            )
            out[-1].start()
    last.wait()
    for copy in out:
        copy.wait()


def prepare_kernel(
    owners, place_ref, length_ref, user_ref, key_ref, value_ref, *rest
):
    history_refs, rest = rest[: SOURCES - 1], rest[SOURCES - 1 :]
    turned_ref, live_ref, back_ref, own, sems = rest
    _, span, width = own.shape
    user, half = role(place_ref[0])
    copies = [
        pltpu.make_async_copy(part_of(history_ref, user, half, width), own.at[kind], sems.at[kind])
        for kind, history_ref in enumerate((key_ref, value_ref))
    ]
    for copy in copies:
        copy.start()
    _, back = orders_of(user_ref[...], back_ref.shape[0])
    back_ref[...] = back
    length = length_ref[user]
    position = lax.broadcasted_iota(jnp.int32, (span, width), 0)
    for index in reversed(range(SOURCES)):
        if index == 0:
            for copy in copies:
                copy.wait()
        history_ref = history_refs[index - 1] if index else own
        at = slice(index * span, (index + 1) * span)
        live = length - source(place_ref[0], index, owners) * span
        turned_ref[:, at] = history_ref[0].T
        value = history_ref[1]
        live_ref[at, :] = jnp.where(position < live, value, jnp.zeros_like(value))


def attend_kernel(rows_now, positions_now, query_ref, keys, values, out_ref):
    blocks, block_rows, width = query_ref.shape
    positions = values.shape[0]
    step_blocks = rows_now // block_rows

    def of_head(array, head):
        return jnp.where(head_mask(array.shape, head), array, jnp.zeros_like(array))

    def step(index, carry):
        here = pl.ds(index * step_blocks, step_blocks)
        query = query_ref[here].reshape(rows_now, width)
        total = jnp.zeros((rows_now, width), jnp.float32)
        for start in range(0, positions, positions_now):
            at = slice(start, start + positions_now)
            for head in range(width // HEAD_DIM):
                half = jnp.dot(
                    of_head(query, head), keys[:, at], preferred_element_type=jnp.float32
                )
                weight = (half + half * jnp.tanh(half)).astype(jnp.bfloat16)
                total += jnp.dot(
                    weight, of_head(values[at, :], head), preferred_element_type=jnp.float32
                )
        out_ref[here] = total.astype(jnp.bfloat16).reshape(step_blocks, block_rows, width)
        return carry

    lax.fori_loop(0, blocks // step_blocks, step, 0)


def finish_kernel(length_ref, back_ref, partial_ref, gate_ref, weight_ref, out_ref):
    rows, width = gate_ref.shape
    sums = {}
    for block in range(partial_ref.shape[0]):
        term = partial_ref[block].astype(jnp.float32)
        sums[role(block)] = sums[role(block)] + term if role(block) in sums else term
    total = jnp.concatenate(
        [jnp.concatenate([sums[user, half] for half in range(2)], axis=1) for user in range(USERS)],
        axis=0,
    )
    row = lax.broadcasted_iota(jnp.int32, (rows, width), 0)
    length = jnp.where(row < rows // USERS, length_ref[0], length_ref[1]).astype(jnp.float32)
    attn = total / length
    square = attn * attn
    mean = jnp.zeros((rows, width), jnp.float32)
    for head in range(width // HEAD_DIM):
        mask = head_mask((rows, width), head)
        summed = jnp.sum(jnp.where(mask, square, 0.0), axis=1, keepdims=True)
        mean = jnp.where(mask, summed * (1.0 / HEAD_DIM), mean)
    normed = attn * lax.rsqrt(mean + 1e-06)
    gated = (normed * gate_ref[...].astype(jnp.float32)).astype(jnp.bfloat16)
    gated = jnp.dot(back_ref[...], gated, preferred_element_type=jnp.float32).astype(jnp.bfloat16)
    for part in range(out_ref.shape[0]):
        out_ref[part] = jnp.dot(
            gated,
            weight_ref[:, part * width : (part + 1) * width],
            preferred_element_type=jnp.float32,
        ).astype(out_ref.dtype)


def add_kernel(cand_ref, term_ref, out_ref):
    total = cand_ref[...].astype(jnp.float32)
    for group in range(term_ref.shape[0]):
        total += term_ref[group].astype(jnp.float32)
    out_ref[...] = total.astype(out_ref.dtype)


def in_hbm(array):
    return pltpu.with_memory_space_constraint(array, pltpu.HBM)


def local(cand_rows, qu_weight, out_weight, keys, values, lengths, cand_user):
    rows, depth = cand_rows.shape
    width = qu_weight.shape[2]
    positions = keys.shape[1]
    groups = lax.axis_size("head")
    owners = lax.axis_size("seq")
    place = jnp.reshape(lax.axis_index("seq"), (1,)).astype(jnp.int32)
    block_rows, lanes = rows // USERS, width // 2

    users = cand_user.reshape(1, rows)
    *shares, copies, kept, weight = pl.pallas_call(
        functools.partial(share_kernel, owners),
        out_shape=[pltpu.HBM((2, positions, lanes), jnp.bfloat16)] * (SOURCES - 1)
        + [
            pltpu.HBM((groups, rows, depth), jnp.bfloat16),
            pltpu.VMEM((rows, depth), jnp.bfloat16),
            pltpu.VMEM(qu_weight.shape, jnp.bfloat16),
        ],
        in_specs=[SMEM] + [HBM] * 5,
        out_specs=[HBM] * SOURCES + [VMEM] * 2,
        scratch_shapes=[
            pltpu.VMEM((1, rows), jnp.int32),
            pltpu.VMEM((rows, depth), jnp.bfloat16),
            pltpu.VMEM((SOURCES - 1, 2, positions, lanes), jnp.bfloat16),
            pltpu.SemaphoreType.DMA((SOURCES - 1, 2)),
            pltpu.SemaphoreType.DMA((groups,)),
            pltpu.SemaphoreType.DMA((3,)),
        ],
        compiler_params=PARAMS,
        name="share",
    )(place, *map(in_hbm, (users, cand_rows, qu_weight, keys, values)))
    history = [
        lax.ppermute(share, "seq", [(s, source(s, index + 1, owners)) for s in range(owners)])
        for index, share in enumerate(shares)
    ]

    cand_parts = lax.all_to_all(copies, "head", 0, 0, tiled=True)
    queries, gates = pl.pallas_call(
        project_kernel,
        out_shape=(
            jax.ShapeDtypeStruct((owners, block_rows, lanes), jnp.bfloat16),
            jax.ShapeDtypeStruct((rows, width), jnp.bfloat16),
        ),
        in_specs=[VMEM] * 2,
        out_specs=(VMEM, VMEM),
        compiler_params=PARAMS,
        name="project",
    )(
        cand_parts,
        weight.reshape(qu_weight.shape[0], 2 * width),
    )
    queries = lax.all_to_all(queries, "seq", 0, 0, tiled=True)
    turned, live, back = pl.pallas_call(
        functools.partial(prepare_kernel, owners),
        out_shape=(
            jax.ShapeDtypeStruct((lanes, SOURCES * positions), jnp.bfloat16),
            jax.ShapeDtypeStruct((SOURCES * positions, lanes), jnp.bfloat16),
            pltpu.VMEM((rows, rows), jnp.bfloat16),
        ),
        in_specs=[SMEM] * 2 + [VMEM] + [HBM] * 2 + [VMEM] * (SOURCES - 1),
        out_specs=(VMEM,) * 3,
        scratch_shapes=[
            pltpu.VMEM((2, positions, lanes), jnp.bfloat16),
            pltpu.SemaphoreType.DMA((2,)),
        ],
        compiler_params=PARAMS,
        name="prepare",
    )(place, lengths, *map(in_hbm, (users, keys, values, *history)))
    totals = pl.pallas_call(
        functools.partial(attend_kernel, 1024, 256),
        out_shape=jax.ShapeDtypeStruct((owners, block_rows, lanes), jnp.bfloat16),
        in_specs=[VMEM] * 3,
        out_specs=VMEM,
        compiler_params=ATTEND_PARAMS,
        name="attend",
    )(queries, turned, live)
    totals = lax.all_to_all(totals, "seq", 0, 0, tiled=True)
    terms = pl.pallas_call(
        finish_kernel,
        out_shape=jax.ShapeDtypeStruct((groups, rows, depth), jnp.bfloat16),
        in_specs=[SMEM] + [VMEM] * 4,
        out_specs=VMEM,
        compiler_params=PARAMS,
        name="finish",
    )(lengths, back, totals, gates, out_weight)
    terms = lax.all_to_all(terms, "head", 0, 0, tiled=True)
    return pl.pallas_call(
        add_kernel,
        out_shape=jax.ShapeDtypeStruct((rows, depth), cand_rows.dtype),
        in_specs=[VMEM, VMEM],
        out_specs=VMEM,
        compiler_params=PARAMS,
        name="add",
    )(kept, terms)


def solution(mesh):
    return jax.shard_map(
        local,
        mesh=mesh,
        in_specs=(
            P(("user", "seq"), "head"),
            P(None, None, "head"),
            P("head", None),
            P("user", "seq", "head"),
            P("user", "seq", "head"),
            P("user"),
            P(("user", "seq")),
        ),
        out_specs=P(("user", "seq"), "head"),
        check_vma=False,
    )
```

```python
import functools

import jax
import jax.numpy as jnp
from jax import lax
from jax.experimental import pallas as pl
from jax.experimental.pallas import tpu as pltpu
from jax.sharding import PartitionSpec as P

HEAD_DIM = 64
USERS = 2
VMEM = pl.BlockSpec(memory_space=pltpu.VMEM)
SMEM = pl.BlockSpec(memory_space=pltpu.SMEM)
HBM = pl.BlockSpec(memory_space=pltpu.HBM)
PARAMS = pltpu.CompilerParams(vmem_limit_bytes=16 * 2**20)
ATTEND_PARAMS = pltpu.CompilerParams(vmem_limit_bytes=24 * 2**20)


SOURCES = 4


def role(place):
    return (place // 4) % 2, (place // 8 + place) % 2


def half_of(member):
    return (member // 4 + member) % 2


def source(place, index, owners):
    if index == 0:
        return place
    if index == 3:
        return place + 1 - 2 * (place % 2)
    step = 4 - 8 * ((place // 4) % 2)
    return (place + (step if index == 1 else -step) + owners) % owners


def head_mask(shape, head):
    lane = lax.broadcasted_iota(jnp.int32, shape, len(shape) - 1)
    return (lane >= head * HEAD_DIM) & (lane < (head + 1) * HEAD_DIM)


def orders_of(users, rows):
    first = lax.broadcasted_iota(jnp.int32, (rows, rows), 0)
    second = lax.broadcasted_iota(jnp.int32, (rows, rows), 1)
    users = jnp.broadcast_to(users, (rows, rows))
    before = jnp.dot(
        users.astype(jnp.bfloat16),
        (first < second).astype(jnp.bfloat16),
        preferred_element_type=jnp.float32,
    ).astype(jnp.int32)
    target = jnp.where(users > 0, rows // USERS + before, second - before)
    order = (target == first).astype(jnp.float32)
    return order.astype(jnp.bfloat16), order.T.astype(jnp.bfloat16)


def project_kernel(cand_ref, weight_ref, query_ref, gate_ref):
    members, share_rows, depth = cand_ref.shape
    slices = members // USERS
    rows = USERS * share_rows
    width = weight_ref.shape[1] // 2
    total = jnp.zeros((rows, 2 * width), jnp.float32)
    for part in range(slices):
        total += jnp.dot(
            jnp.concatenate([cand_ref[part], cand_ref[slices + part]], axis=0),
            weight_ref[part * depth : (part + 1) * depth, :],
            preferred_element_type=jnp.float32,
        )
    projected = (total / (1.0 + jnp.exp(-total))).astype(jnp.bfloat16)
    query = (projected[:, :width].astype(jnp.float32) * (0.5 * HEAD_DIM**-0.5)).astype(
        jnp.bfloat16
    )
    lanes = query_ref.shape[2]
    for member in range(query_ref.shape[0]):
        half = half_of(member)
        query_ref[member] = query[:, half * lanes : (half + 1) * lanes]
    gate_ref[...] = projected[:, width:]


def part_of(history_ref, user, half, lanes):
    return history_ref.at[user, :, pl.ds(pl.multiple_of(half * lanes, lanes), lanes)]


def share_kernel(
    owners, place_ref, user_ref, cand_ref, weight_ref, key_ref, value_ref, *rest
):
    out_refs, rest = rest[: SOURCES - 1], rest[SOURCES - 1 :]
    copy_ref, keep_ref, held_ref, users, rows, parts, sems, copy_sems, own_sems = rest
    lanes = out_refs[0].shape[2]
    first = [
        pltpu.make_async_copy(cand_ref, keep_ref, own_sems.at[0]),
        pltpu.make_async_copy(user_ref, users, own_sems.at[1]),
    ]
    into = []
    for index in range(SOURCES - 1):
        user, half = role(source(place_ref[0], index + 1, owners))
        for kind, history_ref in enumerate((key_ref, value_ref)):
            into.append(
                pltpu.make_async_copy(
                    part_of(history_ref, user, half, lanes),
                    parts.at[index, kind],
                    sems.at[index, kind],
                )
            )
    last = pltpu.make_async_copy(weight_ref, held_ref, own_sems.at[2])
    for copy in first + into + [last]:
        copy.start()
    for copy in first:
        copy.wait()
    order, _ = orders_of(users[...], rows.shape[0])
    rows[...] = jnp.dot(order, keep_ref[...], preferred_element_type=jnp.float32).astype(
        rows.dtype
    )
    out = []
    members, share_rows, _ = copy_ref.shape
    for member in range(members):
        user = member // (members // USERS)
        mine = rows.at[user * share_rows : (user + 1) * share_rows]
        out.append(pltpu.make_async_copy(mine, copy_ref.at[member], copy_sems.at[member]))
        out[-1].start()
    for index, out_ref in enumerate(out_refs):
        for kind in range(2):
            into[2 * index + kind].wait()
            out.append(
                pltpu.make_async_copy(
                    parts.at[index, kind], out_ref.at[kind], sems.at[index, kind]
                )
            )
            out[-1].start()
    last.wait()
    for copy in out:
        copy.wait()


def prepare_kernel(
    owners, place_ref, length_ref, user_ref, key_ref, value_ref, *rest
):
    history_refs, rest = rest[: SOURCES - 1], rest[SOURCES - 1 :]
    turned_ref, live_ref, back_ref, own, sems = rest
    _, span, width = own.shape
    user, half = role(place_ref[0])
    copies = [
        pltpu.make_async_copy(part_of(history_ref, user, half, width), own.at[kind], sems.at[kind])
        for kind, history_ref in enumerate((key_ref, value_ref))
    ]
    for copy in copies:
        copy.start()
    _, back = orders_of(user_ref[...], back_ref.shape[0])
    back_ref[...] = back
    length = length_ref[user]
    position = lax.broadcasted_iota(jnp.int32, (span, width), 0)
    for index in reversed(range(SOURCES)):
        if index == 0:
            for copy in copies:
                copy.wait()
        history_ref = history_refs[index - 1] if index else own
        at = slice(index * span, (index + 1) * span)
        live = length - source(place_ref[0], index, owners) * span
        turned_ref[:, at] = history_ref[0].T
        value = history_ref[1]
        live_ref[at, :] = jnp.where(position < live, value, jnp.zeros_like(value))


def attend_kernel(rows_now, positions_now, query_ref, keys, values, out_ref):
    blocks, block_rows, width = query_ref.shape
    positions = values.shape[0]
    step_blocks = rows_now // block_rows

    def of_head(array, head):
        return jnp.where(head_mask(array.shape, head), array, jnp.zeros_like(array))

    def step(index, carry):
        here = pl.ds(index * step_blocks, step_blocks)
        query = query_ref[here].reshape(rows_now, width)
        total = jnp.zeros((rows_now, width), jnp.float32)
        for start in range(0, positions, positions_now):
            at = slice(start, start + positions_now)
            for head in range(width // HEAD_DIM):
                half = jnp.dot(
                    of_head(query, head), keys[:, at], preferred_element_type=jnp.float32
                )
                weight = (half + half * jnp.tanh(half)).astype(jnp.bfloat16)
                total += jnp.dot(
                    weight, of_head(values[at, :], head), preferred_element_type=jnp.float32
                )
        out_ref[here] = total.astype(jnp.bfloat16).reshape(step_blocks, block_rows, width)
        return carry

    lax.fori_loop(0, blocks // step_blocks, step, 0)


def finish_kernel(place_ref, length_ref, partial_ref, gate_ref, weight_ref, out_ref):
    rows, width = gate_ref.shape
    sums = {}
    for member in range(partial_ref.shape[0]):
        term = partial_ref[member].astype(jnp.float32)
        half = half_of(member)
        sums[half] = sums[half] + term if half in sums else term
    total = jnp.concatenate([sums[0], sums[1]], axis=1)
    user, _ = role(place_ref[0])
    length = jnp.full((rows, width), length_ref[user], jnp.int32).astype(jnp.float32)
    attn = total / length
    square = attn * attn
    mean = jnp.zeros((rows, width), jnp.float32)
    for head in range(width // HEAD_DIM):
        mask = head_mask((rows, width), head)
        summed = jnp.sum(jnp.where(mask, square, 0.0), axis=1, keepdims=True)
        mean = jnp.where(mask, summed * (1.0 / HEAD_DIM), mean)
    normed = attn * lax.rsqrt(mean + 1e-06)
    gated = (normed * gate_ref[...].astype(jnp.float32)).astype(jnp.bfloat16)
    members, share_rows, depth = out_ref.shape
    slices = members // USERS
    for part in range(slices):
        term = jnp.dot(
            gated,
            weight_ref[:, part * depth : (part + 1) * depth],
            preferred_element_type=jnp.float32,
        ).astype(out_ref.dtype)
        for block in range(USERS):
            out_ref[block * slices + part] = term[block * share_rows : (block + 1) * share_rows]


def add_kernel(cand_ref, back_ref, term_ref, out_ref):
    slices = term_ref.shape[0] // USERS
    total = cand_ref[...].astype(jnp.float32)
    for part in range(slices):
        term = jnp.concatenate([term_ref[part], term_ref[slices + part]], axis=0)
        total += jnp.dot(back_ref[...], term, preferred_element_type=jnp.float32)
    out_ref[...] = total.astype(out_ref.dtype)


def in_hbm(array):
    return pltpu.with_memory_space_constraint(array, pltpu.HBM)


def local(cand_rows, qu_weight, out_weight, keys, values, lengths, cand_user):
    rows, depth = cand_rows.shape
    width = qu_weight.shape[2]
    positions = keys.shape[1]
    groups = lax.axis_size("head")
    owners = lax.axis_size("seq")
    place = jnp.reshape(lax.axis_index("seq"), (1,)).astype(jnp.int32)
    block_rows, lanes = rows // USERS, width // 2

    users = cand_user.reshape(1, rows)
    *shares, copies, kept, weight = pl.pallas_call(
        functools.partial(share_kernel, owners),
        out_shape=[pltpu.HBM((2, positions, lanes), jnp.bfloat16)] * (SOURCES - 1)
        + [
            pltpu.HBM((USERS * groups, block_rows, depth), jnp.bfloat16),
            pltpu.VMEM((rows, depth), jnp.bfloat16),
            pltpu.VMEM(qu_weight.shape, jnp.bfloat16),
        ],
        in_specs=[SMEM] + [HBM] * 5,
        out_specs=[HBM] * SOURCES + [VMEM] * 2,
        scratch_shapes=[
            pltpu.VMEM((1, rows), jnp.int32),
            pltpu.VMEM((rows, depth), jnp.bfloat16),
            pltpu.VMEM((SOURCES - 1, 2, positions, lanes), jnp.bfloat16),
            pltpu.SemaphoreType.DMA((SOURCES - 1, 2)),
            pltpu.SemaphoreType.DMA((USERS * groups,)),
            pltpu.SemaphoreType.DMA((3,)),
        ],
        compiler_params=PARAMS,
        name="share",
    )(place, *map(in_hbm, (users, cand_rows, qu_weight, keys, values)))
    history = [
        lax.ppermute(share, "seq", [(s, source(s, index + 1, owners)) for s in range(owners)])
        for index, share in enumerate(shares)
    ]

    pairs = [
        [group * owners + first + 4 * user for user in range(USERS) for group in range(groups)]
        for first in range(owners)
        if role(first)[0] == 0
    ]
    of_user = [[s for s in range(owners) if role(s)[0] == user] for user in range(USERS)]

    def over_pair(array):
        return lax.all_to_all(
            array, ("head", "seq"), 0, 0, tiled=True, axis_index_groups=pairs
        )

    def over_user(array):
        return lax.all_to_all(array, "seq", 0, 0, tiled=True, axis_index_groups=of_user)

    cand_parts = over_pair(copies)
    queries, gates = pl.pallas_call(
        project_kernel,
        out_shape=(
            jax.ShapeDtypeStruct((owners // USERS, rows, lanes), jnp.bfloat16),
            jax.ShapeDtypeStruct((rows, width), jnp.bfloat16),
        ),
        in_specs=[VMEM] * 2,
        out_specs=(VMEM, VMEM),
        compiler_params=PARAMS,
        name="project",
    )(
        cand_parts,
        weight.reshape(qu_weight.shape[0], 2 * width),
    )
    queries = over_user(queries)
    turned, live, back = pl.pallas_call(
        functools.partial(prepare_kernel, owners),
        out_shape=(
            jax.ShapeDtypeStruct((lanes, SOURCES * positions), jnp.bfloat16),
            jax.ShapeDtypeStruct((SOURCES * positions, lanes), jnp.bfloat16),
            pltpu.VMEM((rows, rows), jnp.bfloat16),
        ),
        in_specs=[SMEM] * 2 + [VMEM] + [HBM] * 2 + [VMEM] * (SOURCES - 1),
        out_specs=(VMEM,) * 3,
        scratch_shapes=[
            pltpu.VMEM((2, positions, lanes), jnp.bfloat16),
            pltpu.SemaphoreType.DMA((2,)),
        ],
        compiler_params=PARAMS,
        name="prepare",
    )(place, lengths, *map(in_hbm, (users, keys, values, *history)))
    totals = pl.pallas_call(
        functools.partial(attend_kernel, 1024, 256),
        out_shape=jax.ShapeDtypeStruct((owners // USERS, rows, lanes), jnp.bfloat16),
        in_specs=[VMEM] * 3,
        out_specs=VMEM,
        compiler_params=ATTEND_PARAMS,
        name="attend",
    )(queries, turned, live)
    totals = over_user(totals)
    terms = pl.pallas_call(
        finish_kernel,
        out_shape=jax.ShapeDtypeStruct((USERS * groups, block_rows, depth), jnp.bfloat16),
        in_specs=[SMEM] * 2 + [VMEM] * 3,
        out_specs=VMEM,
        compiler_params=PARAMS,
        name="finish",
    )(place, lengths, totals, gates, out_weight)
    return pl.pallas_call(
        add_kernel,
        out_shape=jax.ShapeDtypeStruct((rows, depth), cand_rows.dtype),
        in_specs=[VMEM] * 3,
        out_specs=VMEM,
        compiler_params=PARAMS,
        name="add",
    )(kept, back, over_pair(terms))


def solution(mesh):
    return jax.shard_map(
        local,
        mesh=mesh,
        in_specs=(
            P(("user", "seq"), "head"),
            P(None, None, "head"),
            P("head", None),
            P("user", "seq", "head"),
            P("user", "seq", "head"),
            P("user"),
            P(("user", "seq")),
        ),
        out_specs=P(("user", "seq"), "head"),
        check_vma=False,
    )
```

```python
import functools

import jax
import jax.numpy as jnp
from jax import lax
from jax.experimental import pallas as pl
from jax.experimental.pallas import tpu as pltpu
from jax.sharding import PartitionSpec as P

HEAD_DIM = 64
USERS = 2
VMEM = pl.BlockSpec(memory_space=pltpu.VMEM)
SMEM = pl.BlockSpec(memory_space=pltpu.SMEM)
HBM = pl.BlockSpec(memory_space=pltpu.HBM)
PARAMS = pltpu.CompilerParams(vmem_limit_bytes=16 * 2**20)
ATTEND_PARAMS = pltpu.CompilerParams(vmem_limit_bytes=24 * 2**20)


SOURCES = 4


def role(place):
    return (place // 4) % 2, (place // 8 + place) % 2


def source(place, index, owners):
    if index == 0:
        return place
    if index == 3:
        return place + 1 - 2 * (place % 2)
    step = 4 - 8 * ((place // 4) % 2)
    return (place + (step if index == 2 else -step) + owners) % owners


def head_mask(shape, head):
    lane = lax.broadcasted_iota(jnp.int32, shape, len(shape) - 1)
    return (lane >= head * HEAD_DIM) & (lane < (head + 1) * HEAD_DIM)


def orders_of(users, rows):
    first = lax.broadcasted_iota(jnp.int32, (rows, rows), 0)
    second = lax.broadcasted_iota(jnp.int32, (rows, rows), 1)
    users = jnp.broadcast_to(users, (rows, rows))
    before = jnp.dot(
        users.astype(jnp.bfloat16),
        (first < second).astype(jnp.bfloat16),
        preferred_element_type=jnp.float32,
    ).astype(jnp.int32)
    target = jnp.where(users > 0, rows // USERS + before, second - before)
    order = (target == first).astype(jnp.float32)
    return order.astype(jnp.bfloat16), order.T.astype(jnp.bfloat16)


def project_kernel(cand_ref, weight_ref, query_ref, gate_ref):
    slices, rows, depth = cand_ref.shape
    width = weight_ref.shape[1] // 2
    total = jnp.zeros((rows, 2 * width), jnp.float32)
    for part in range(slices):
        total += jnp.dot(
            cand_ref[part],
            weight_ref[part * depth : (part + 1) * depth, :],
            preferred_element_type=jnp.float32,
        )
    projected = (total / (1.0 + jnp.exp(-total))).astype(jnp.bfloat16)
    query = (projected[:, :width].astype(jnp.float32) * (0.5 * HEAD_DIM**-0.5)).astype(
        jnp.bfloat16
    )
    _, block_rows, lanes = query_ref.shape
    for owner in range(query_ref.shape[0]):
        user, half = role(owner)
        query_ref[owner] = query[
            user * block_rows : (user + 1) * block_rows, half * lanes : (half + 1) * lanes
        ]
    gate_ref[...] = projected[:, width:]


def part_of(history_ref, user, half, lanes):
    return history_ref.at[user, :, pl.ds(pl.multiple_of(half * lanes, lanes), lanes)]


def share_kernel(
    owners, place_ref, user_ref, cand_ref, weight_ref, key_ref, value_ref, *rest
):
    out_refs, rest = rest[: SOURCES - 1], rest[SOURCES - 1 :]
    copy_ref, keep_ref, held_ref, users, rows, parts, sems, copy_sems, own_sems = rest
    lanes = out_refs[0].shape[2]
    first = [
        pltpu.make_async_copy(cand_ref, keep_ref, own_sems.at[0]),
        pltpu.make_async_copy(user_ref, users, own_sems.at[1]),
    ]
    into = []
    for index in range(SOURCES - 1):
        user, half = role(source(place_ref[0], index + 1, owners))
        for kind, history_ref in enumerate((key_ref, value_ref)):
            into.append(
                pltpu.make_async_copy(
                    part_of(history_ref, user, half, lanes),
                    parts.at[index, kind],
                    sems.at[index, kind],
                )
            )
    last = pltpu.make_async_copy(weight_ref, held_ref, own_sems.at[2])
    for copy in first + into + [last]:
        copy.start()
    for copy in first:
        copy.wait()
    order, _ = orders_of(users[...], rows.shape[0])
    rows[...] = jnp.dot(order, keep_ref[...], preferred_element_type=jnp.float32).astype(
        rows.dtype
    )
    out = []
    for group in range(copy_ref.shape[0]):
        out.append(pltpu.make_async_copy(rows, copy_ref.at[group], copy_sems.at[group]))
        out[-1].start()
    for index, out_ref in enumerate(out_refs):
        for kind in range(2):
            into[2 * index + kind].wait()
            out.append(
                pltpu.make_async_copy(
                    parts.at[index, kind], out_ref.at[kind], sems.at[index, kind]
                )
            )
            out[-1].start()
    last.wait()
    for copy in out:
        copy.wait()


def prepare_kernel(
    owners, place_ref, length_ref, user_ref, key_ref, value_ref, *rest
):
    history_refs, rest = rest[: SOURCES - 1], rest[SOURCES - 1 :]
    turned_ref, live_ref, back_ref, own, sems = rest
    _, span, width = own.shape
    user, half = role(place_ref[0])
    copies = [
        pltpu.make_async_copy(part_of(history_ref, user, half, width), own.at[kind], sems.at[kind])
        for kind, history_ref in enumerate((key_ref, value_ref))
    ]
    for copy in copies:
        copy.start()
    _, back = orders_of(user_ref[...], back_ref.shape[0])
    back_ref[...] = back
    length = length_ref[user]
    position = lax.broadcasted_iota(jnp.int32, (span, width), 0)
    for index in reversed(range(SOURCES)):
        if index == 0:
            for copy in copies:
                copy.wait()
        history_ref = history_refs[index - 1] if index else own
        at = slice(index * span, (index + 1) * span)
        live = length - source(place_ref[0], index, owners) * span
        turned_ref[:, at] = history_ref[0].T
        value = history_ref[1]
        live_ref[at, :] = jnp.where(position < live, value, jnp.zeros_like(value))


def attend_kernel(rows_now, positions_now, query_ref, keys, values, out_ref):
    blocks, block_rows, width = query_ref.shape
    positions = values.shape[0]
    step_blocks = rows_now // block_rows

    def of_head(array, head):
        return jnp.where(head_mask(array.shape, head), array, jnp.zeros_like(array))

    def step(index, carry):
        here = pl.ds(index * step_blocks, step_blocks)
        query = query_ref[here].reshape(rows_now, width)
        total = jnp.zeros((rows_now, width), jnp.float32)
        for start in range(0, positions, positions_now):
            at = slice(start, start + positions_now)
            for head in range(width // HEAD_DIM):
                half = jnp.dot(
                    of_head(query, head), keys[:, at], preferred_element_type=jnp.float32
                )
                weight = (half + half * jnp.tanh(half)).astype(jnp.bfloat16)
                total += jnp.dot(
                    weight, of_head(values[at, :], head), preferred_element_type=jnp.float32
                )
        out_ref[here] = total.astype(jnp.bfloat16).reshape(step_blocks, block_rows, width)
        return carry

    lax.fori_loop(0, blocks // step_blocks, step, 0)


def finish_kernel(length_ref, back_ref, partial_ref, gate_ref, weight_ref, out_ref):
    rows, width = gate_ref.shape
    sums = {}
    for block in range(partial_ref.shape[0]):
        term = partial_ref[block].astype(jnp.float32)
        sums[role(block)] = sums[role(block)] + term if role(block) in sums else term
    total = jnp.concatenate(
        [jnp.concatenate([sums[user, half] for half in range(2)], axis=1) for user in range(USERS)],
        axis=0,
    )
    row = lax.broadcasted_iota(jnp.int32, (rows, width), 0)
    length = jnp.where(row < rows // USERS, length_ref[0], length_ref[1]).astype(jnp.float32)
    attn = total / length
    square = attn * attn
    mean = jnp.zeros((rows, width), jnp.float32)
    for head in range(width // HEAD_DIM):
        mask = head_mask((rows, width), head)
        summed = jnp.sum(jnp.where(mask, square, 0.0), axis=1, keepdims=True)
        mean = jnp.where(mask, summed * (1.0 / HEAD_DIM), mean)
    normed = attn * lax.rsqrt(mean + 1e-06)
    gated = (normed * gate_ref[...].astype(jnp.float32)).astype(jnp.bfloat16)
    gated = jnp.dot(back_ref[...], gated, preferred_element_type=jnp.float32).astype(jnp.bfloat16)
    for part in range(out_ref.shape[0]):
        out_ref[part] = jnp.dot(
            gated,
            weight_ref[:, part * width : (part + 1) * width],
            preferred_element_type=jnp.float32,
        ).astype(out_ref.dtype)


def add_kernel(cand_ref, term_ref, out_ref):
    total = cand_ref[...].astype(jnp.float32)
    for group in range(term_ref.shape[0]):
        total += term_ref[group].astype(jnp.float32)
    out_ref[...] = total.astype(out_ref.dtype)


def in_hbm(array):
    return pltpu.with_memory_space_constraint(array, pltpu.HBM)


def local(cand_rows, qu_weight, out_weight, keys, values, lengths, cand_user):
    rows, depth = cand_rows.shape
    width = qu_weight.shape[2]
    positions = keys.shape[1]
    groups = lax.axis_size("head")
    owners = lax.axis_size("seq")
    place = jnp.reshape(lax.axis_index("seq"), (1,)).astype(jnp.int32)
    block_rows, lanes = rows // USERS, width // 2

    users = cand_user.reshape(1, rows)
    *shares, copies, kept, weight = pl.pallas_call(
        functools.partial(share_kernel, owners),
        out_shape=[pltpu.HBM((2, positions, lanes), jnp.bfloat16)] * (SOURCES - 1)
        + [
            pltpu.HBM((groups, rows, depth), jnp.bfloat16),
            pltpu.VMEM((rows, depth), jnp.bfloat16),
            pltpu.VMEM(qu_weight.shape, jnp.bfloat16),
        ],
        in_specs=[SMEM] + [HBM] * 5,
        out_specs=[HBM] * SOURCES + [VMEM] * 2,
        scratch_shapes=[
            pltpu.VMEM((1, rows), jnp.int32),
            pltpu.VMEM((rows, depth), jnp.bfloat16),
            pltpu.VMEM((SOURCES - 1, 2, positions, lanes), jnp.bfloat16),
            pltpu.SemaphoreType.DMA((SOURCES - 1, 2)),
            pltpu.SemaphoreType.DMA((groups,)),
            pltpu.SemaphoreType.DMA((3,)),
        ],
        compiler_params=PARAMS,
        name="share",
    )(place, *map(in_hbm, (users, cand_rows, qu_weight, keys, values)))
    history = [
        lax.ppermute(share, "seq", [(s, source(s, index + 1, owners)) for s in range(owners)])
        for index, share in enumerate(shares)
    ]

    cand_parts = lax.all_to_all(copies, "head", 0, 0, tiled=True)
    queries, gates = pl.pallas_call(
        project_kernel,
        out_shape=(
            jax.ShapeDtypeStruct((owners, block_rows, lanes), jnp.bfloat16),
            jax.ShapeDtypeStruct((rows, width), jnp.bfloat16),
        ),
        in_specs=[VMEM] * 2,
        out_specs=(VMEM, VMEM),
        compiler_params=PARAMS,
        name="project",
    )(
        cand_parts,
        weight.reshape(qu_weight.shape[0], 2 * width),
    )
    queries = lax.all_to_all(queries, "seq", 0, 0, tiled=True)
    turned, live, back = pl.pallas_call(
        functools.partial(prepare_kernel, owners),
        out_shape=(
            jax.ShapeDtypeStruct((lanes, SOURCES * positions), jnp.bfloat16),
            jax.ShapeDtypeStruct((SOURCES * positions, lanes), jnp.bfloat16),
            pltpu.VMEM((rows, rows), jnp.bfloat16),
        ),
        in_specs=[SMEM] * 2 + [VMEM] + [HBM] * 2 + [VMEM] * (SOURCES - 1),
        out_specs=(VMEM,) * 3,
        scratch_shapes=[
            pltpu.VMEM((2, positions, lanes), jnp.bfloat16),
            pltpu.SemaphoreType.DMA((2,)),
        ],
        compiler_params=PARAMS,
        name="prepare",
    )(place, lengths, *map(in_hbm, (users, keys, values, *history)))
    totals = pl.pallas_call(
        functools.partial(attend_kernel, 1024, 256),
        out_shape=jax.ShapeDtypeStruct((owners, block_rows, lanes), jnp.bfloat16),
        in_specs=[VMEM] * 3,
        out_specs=VMEM,
        compiler_params=ATTEND_PARAMS,
        name="attend",
    )(queries, turned, live)
    totals = lax.all_to_all(totals, "seq", 0, 0, tiled=True)
    terms = pl.pallas_call(
        finish_kernel,
        out_shape=jax.ShapeDtypeStruct((groups, rows, depth), jnp.bfloat16),
        in_specs=[SMEM] + [VMEM] * 4,
        out_specs=VMEM,
        compiler_params=PARAMS,
        name="finish",
    )(lengths, back, totals, gates, out_weight)
    terms = lax.all_to_all(terms, "head", 0, 0, tiled=True)
    return pl.pallas_call(
        add_kernel,
        out_shape=jax.ShapeDtypeStruct((rows, depth), cand_rows.dtype),
        in_specs=[VMEM, VMEM],
        out_specs=VMEM,
        compiler_params=PARAMS,
        name="add",
    )(kept, terms)


def solution(mesh):
    return jax.shard_map(
        local,
        mesh=mesh,
        in_specs=(
            P(("user", "seq"), "head"),
            P(None, None, "head"),
            P("head", None),
            P("user", "seq", "head"),
            P("user", "seq", "head"),
            P("user"),
            P(("user", "seq")),
        ),
        out_specs=P(("user", "seq"), "head"),
        check_vma=False,
    )
```
